128 devices in a mesh: row: 8 (over x, y_hi), col: 16 (over y_lo, z, core).
Axes of the slice: x: 4, y: 4 (y_hi: 2, y_lo: 2; y = y_hi * 2 + y_lo), z: 4, core: 2. Of those that a mesh axis runs over, the one named last changes fastest.
Arguments:
- field: float32 [256, 1024, 128], P('row', 'col'), may hold values from -6 to 6
- expand_weight: float32 [128, 512], replicated, may hold values from -0.5 to 0.5
- depth_weight: float32 [9, 512], replicated, may hold values from -2 to 2
- project_weight: float32 [512, 128], replicated, may hold values from -0.25 to 0.25
- qkv_weight: float32 [128, 384], replicated, may hold values from -0.5 to 0.5
- out_weight: float32 [128, 128], replicated, may hold values from -0.5 to 0.5
- pos_bias: float32 [4, 64, 64], replicated, may hold values from -4 to 300
- cotangent: float32 [256, 1024, 128], P('row', 'col'), may hold values from -6 to 6
Outputs:
- block_out: float32 [256, 1024, 128], P('row', 'col')
- grad_field: float32 [256, 1024, 128], P('row', 'col')
- grad_expand: float32 [128, 512], replicated
- grad_depth: float32 [9, 512], replicated
- grad_project: float32 [512, 128], replicated
- grad_qkv: float32 [128, 384], replicated
- grad_out: float32 [128, 128], replicated
- grad_bias: float32 [4, 64, 64], replicated
The draws below stay inside these ranges and needn't reach their ends.
All inputs are finite; a program needn't handle non-finite values.
Results may differ from the reference program's by a relative error of at most 0.00013.
Values sent between devices are 32-bit elements; how exact they have to be, the bound alone decides.
No kernel may reach another device: no remote copies, remote signals or barrier semaphores. Data moves between devices by JAX's collectives and lax.ppermute only.
A program may use at most 128 MiB of HBM per device.

```python
import jax
import jax.numpy as jnp
from jax import lax

C = 128
E = 512
HEADS = 4
GRID = 8
POS = 64
NH = 256
NW = 1024


def draw_pos_bias(key, part):
    key = jax.random.fold_in(key, 11)
    base_key = jax.random.fold_in(key, 0)
    base = jax.random.uniform(base_key, (HEADS, POS, POS), jnp.float32, -4.0, 4.0)
    return base


def shard_levels(rng, shape, pieces, smallest, high):
    level = 1.0
    for dim, blocks in pieces:
        heights = jax.random.uniform(jax.random.fold_in(jax.random.fold_in(rng, 6), dim), (blocks,), jnp.float32, smallest / len(pieces), high / len(pieces))
        level = level * jnp.repeat(jnp.exp(heights), shape[dim] // blocks).reshape((-1,) + (1,) * (len(shape) - 1 - dim))
    return level


def noise(key, shape, scale, bound, pieces=(), held_as=jnp.bfloat16):
    loudness = shard_levels(key, shape, pieces, -0.22, 0.18) if pieces else 1.0
    values = jax.random.normal(key, shape, jnp.float32) * scale * loudness
    return jnp.minimum(jnp.maximum(values, -bound), bound).astype(held_as)


def setup_inputs(seed: int = 0) -> dict:
    seeds = jax.random.split(jax.random.key(seed), 9)
    field = noise(seeds[0], (NH, NW, C), 1.0, 6.0, ((0, 8), (1, 16)), jnp.float32)
    expand_weight = noise(seeds[1], (C, E), C ** -0.5, 0.5, (), jnp.float32)
    depth_weight = noise(seeds[2], (9, E), 9 ** -0.5, 2.0, (), jnp.float32)
    project_weight = noise(seeds[3], (E, C), E ** -0.5, 0.25, (), jnp.float32)
    qkv_weight = noise(seeds[4], (C, 3 * C), C ** -0.5, 0.5, (), jnp.float32)
    out_weight = noise(seeds[5], (C, C), C ** -0.5, 0.5, (), jnp.float32)
    pos_bias = draw_pos_bias(jax.random.fold_in(seeds[8], 71), 0)
    cotangent = noise(seeds[7], (NH, NW, C), 1.0, 6.0, ((0, 8), (1, 16)), jnp.float32)
    return {"field": field, "expand_weight": expand_weight, "depth_weight": depth_weight, "project_weight": project_weight, "qkv_weight": qkv_weight, "out_weight": out_weight, "pos_bias": pos_bias, "cotangent": cotangent}


def layer_norm(values):
    center = values - lax.optimization_barrier(jnp.mean(values, axis=-1, keepdims=True))
    spread = lax.optimization_barrier(jnp.mean(center * center, axis=-1, keepdims=True))
    return center * lax.rsqrt(spread + 1e-05)

def expand_part(tile, expand_weight):
    normed = layer_norm(tile)
    return jax.nn.gelu(jnp.einsum('ijc,cf->ijf', normed, expand_weight, precision=lax.Precision.HIGHEST))

def project_part(depth_out, project_weight):
    return jnp.einsum('ijf,fc->ijc', jax.nn.gelu(depth_out), project_weight, precision=lax.Precision.HIGHEST)

def depthwise(padded, depth_weight, out_rows, out_cols):
    total = jnp.zeros((out_rows, out_cols, padded.shape[2]), jnp.float32)
    for row_shift in range(3):
        for col_shift in range(3):
            total = total + padded[row_shift:row_shift + out_rows, col_shift:col_shift + out_cols] * depth_weight[3 * row_shift + col_shift]
    return total

def attend(grouped, qkv_weight, out_weight, pos_bias):
    groups, places, channels = grouped.shape
    head_count = pos_bias.shape[0]
    head_size = channels // head_count
    normed = layer_norm(grouped)
    packed = jnp.einsum('gpc,cf->gpf', normed, qkv_weight, precision=lax.Precision.HIGHEST)
    query_rows = packed[..., :channels].reshape(groups, places, head_count, head_size)
    key_rows = packed[..., channels:2 * channels].reshape(groups, places, head_count, head_size)
    value_rows = packed[..., 2 * channels:].reshape(groups, places, head_count, head_size)
    scores = jnp.einsum('gphd,gqhd->ghpq', query_rows, key_rows, precision=lax.Precision.HIGHEST) * head_size ** (-0.5)
    scores = scores + pos_bias[None]
    weights = jax.nn.softmax(scores, axis=-1)
    mixture = jnp.einsum('ghpq,gqhd->gphd', weights, value_rows, precision=lax.Precision.HIGHEST).reshape(groups, places, channels)
    return jnp.einsum('gpc,cf->gpf', mixture, out_weight, precision=lax.Precision.HIGHEST)

def forward(field, expand_weight, depth_weight, project_weight, qkv_weight, out_weight, pos_bias):
    hidden = expand_part(field, expand_weight)
    padded = jnp.pad(hidden, ((1, 1), (1, 1), (0, 0)))
    depth_out = depthwise(padded, depth_weight, NH, NW)
    mixed = field + project_part(depth_out, project_weight)
    grouped = mixed.reshape(GRID, NH // GRID, GRID, NW // GRID, C).transpose(1, 3, 0, 2, 4).reshape(-1, GRID * GRID, C)
    attended = attend(grouped, qkv_weight, out_weight, pos_bias)
    placed = attended.reshape(NH // GRID, NW // GRID, GRID, GRID, C).transpose(2, 0, 3, 1, 4).reshape(NH, NW, C)
    return mixed + placed

def reference(field, expand_weight, depth_weight, project_weight, qkv_weight, out_weight, pos_bias, cotangent):
    result, pullback = jax.vjp(forward, field, expand_weight, depth_weight, project_weight, qkv_weight, out_weight, pos_bias)
    grads = pullback(cotangent)
    return (result, grads[0], grads[1], grads[2], grads[3], grads[4], grads[5], grads[6])
```

```python
import functools

import jax
import jax.numpy as jnp
from jax import lax
from jax.experimental import pallas as pl
from jax.experimental.pallas import tpu as pltpu
from jax.sharding import Mesh, PartitionSpec as P

GRID = 8
HEADS = 4
ALL = ("row", "ch", "core")
COLS = ("ch", "core")
PAIRS = ("row", "ch")
K0 = 0.7978845608028654
K1 = K0 * 0.044715
F32 = jnp.float32
BF16 = jnp.bfloat16
NN = (((1,), (0,)), ((), ()))
NT = (((1,), (1,)), ((), ()))
TN = (((0,), (0,)), ((), ()))


def split(values):
    high = values.astype(BF16)
    return high, (values - high.astype(F32)).astype(BF16)


def dot(a, b, dims):
    return lax.dot_general(a, b, dims, preferred_element_type=F32)


def dot3(a, b, dims):
    a_high, a_low = a if isinstance(a, tuple) else split(a)
    b_high, b_low = b if isinstance(b, tuple) else split(b)
    return dot(a_high, b_high, dims) + (dot(a_low, b_high, dims) + dot(a_high, b_low, dims))


def normalize(values):
    center = values - jnp.mean(values, axis=-1, keepdims=True)
    spread = jnp.mean(center * center, axis=-1, keepdims=True)
    scale = lax.rsqrt(spread + 1e-05)
    return center * scale, scale


def normalize_back(grad, normed, scale):
    grad_mean = jnp.mean(grad, axis=-1, keepdims=True)
    along = jnp.mean(grad * normed, axis=-1, keepdims=True)
    return scale * (grad - grad_mean - normed * along)


def gate(values):
    return 0.5 + 0.5 * jnp.tanh(values * (K0 + K1 * (values * values)))


def gelu(values):
    return values * gate(values)


def gelu_slope(values, gated):
    return gated + 2.0 * values * (gated - gated * gated) * (K0 + (3.0 * K1) * (values * values))


def call(body, grid, in_specs, out_specs, out_shape, scratch=(), flops=0, bytes_accessed=0, limit=56):
    return pl.pallas_call(
        body,
        grid=grid,
        in_specs=in_specs,
        out_specs=out_specs,
        out_shape=out_shape,
        scratch_shapes=list(scratch),
        compiler_params=pltpu.CompilerParams(vmem_limit_bytes=limit * 2**20),
        cost_estimate=pl.CostEstimate(
            flops=flops, bytes_accessed=bytes_accessed, transcendentals=0
        ),
    )


def shape(*dims):
    return jax.ShapeDtypeStruct(dims, F32)


def whole(*dims):
    return pl.BlockSpec(dims, lambda *_: (0,) * len(dims))


def rows(*dims):
    return pl.BlockSpec(dims, lambda i: (i,) + (0,) * (len(dims) - 1))


def expand_body(field_ref, weight_ref, pre_ref, hidden_ref):
    normed, _ = normalize(field_ref[...])
    pre = dot3(normed, weight_ref[...], NN)
    pre_ref[...] = pre
    hidden_ref[...] = gelu(pre)


def expand(field, weight):
    tokens, channels = field.shape
    wide = weight.shape[1]
    step = 256
    return call(
        expand_body,
        (tokens // step,),
        [rows(step, channels), whole(channels, wide)],
        [rows(step, wide), rows(step, wide)],
        [shape(tokens, wide), shape(tokens, wide)],
        flops=6 * tokens * channels * wide,
        bytes_accessed=4 * tokens * (channels + 2 * wide),
    )(field, weight)


def fill_padded(padded, step, last, body_ref, before_ref, after_ref, top, bottom, left, right):
    count, cols = body_ref.shape[0], body_ref.shape[1]
    padded[1 : 1 + count, 8 : 8 + cols, :] = body_ref[...]

    @pl.when(step == 0)
    def _():
        padded[0, 8 : 8 + cols, :] = top[...]

    @pl.when(step > 0)
    def _():
        padded[0, 8 : 8 + cols, :] = before_ref[0]

    @pl.when(step == last)
    def _():
        padded[count + 1, 8 : 8 + cols, :] = bottom[...]

    @pl.when(step < last)
    def _():
        padded[count + 1, 8 : 8 + cols, :] = after_ref[0]

    for k in range(count + 2):
        padded[k, 7:8, :] = left[pl.ds(step * count + k, 1), :]
        padded[k, 8 + cols : 9 + cols, :] = right[pl.ds(step * count + k, 1), :]


def project_body(
    hidden_ref, before_ref, after_ref, top_ref, bottom_ref, left_ref, right_ref, field_ref,
    expand_ref, depth_ref, weight_ref, mixed_ref, depth_out_ref,
    padded, top, bottom, left, right,
):
    step = pl.program_id(0)
    last = pl.num_programs(0) - 1

    @pl.when(step == 0)
    def _():
        weight = split(expand_ref[...])
        for source, target in (
            (top_ref, top), (bottom_ref, bottom), (left_ref, left), (right_ref, right)
        ):
            target[...] = gelu(dot3(normalize(source[...])[0], weight, NN))

    fill_padded(padded, step, last, hidden_ref, before_ref, after_ref, top, bottom, left, right)
    count, cols, wide = hidden_ref.shape
    for i in range(count):
        for lane in range(0, wide, 128):
            lanes = slice(lane, lane + 128)
            total = None
            for p in range(3):
                for q in range(3):
                    term = padded[i + p, 7 + q : 7 + q + cols, lanes] * depth_ref[3 * p + q : 3 * p + q + 1, lanes]
                    total = term if total is None else total + term
            depth_out_ref[i, :, lanes] = total
    activated = gelu(depth_out_ref[...].reshape(count * cols, wide))
    mixed = dot3(activated, weight_ref[...], NN) + field_ref[...].reshape(count * cols, -1)
    for i in range(count):
        for k in range(cols // 8):
            start = i * cols + 8 * k
            mixed_ref[0, k, i] = mixed[start : start + 8]


def neighbours(count, cols, wide, total):
    return [
        pl.BlockSpec((count, cols, wide), lambda i: (i, 0, 0)),
        pl.BlockSpec((1, cols, wide), lambda i: (jnp.maximum(count * i - 1, 0), 0, 0)),
        pl.BlockSpec((1, cols, wide), lambda i: (jnp.minimum(count * i + count, total - 1), 0, 0)),
    ]


def project(hidden, halo, field, expand_weight, depth_weight, weight):
    tile_rows, tile_cols, channels = field.shape
    wide = hidden.shape[2]
    count = tile_rows // GRID
    edge = tile_rows + 2
    return call(
        project_body,
        (GRID,),
        neighbours(count, tile_cols, wide, tile_rows)
        + [whole(tile_cols, channels)] * 2
        + [whole(edge, channels)] * 2
        + [rows(count, tile_cols, channels), whole(channels, wide), whole(9, wide), whole(wide, channels)],
        [rows(1, tile_cols // 8, count, 8, channels), rows(count, tile_cols, wide)],
        [shape(GRID, tile_cols // 8, count, 8, channels), shape(tile_rows, tile_cols, wide)],
        scratch=[
            pltpu.VMEM((count + 2, tile_cols + 16, wide), F32),
            pltpu.VMEM((tile_cols, wide), F32),
            pltpu.VMEM((tile_cols, wide), F32),
            pltpu.VMEM((edge, wide), F32),
            pltpu.VMEM((edge, wide), F32),
        ],
        flops=6 * tile_rows * tile_cols * channels * wide,
        bytes_accessed=4 * tile_rows * tile_cols * (3 * wide + 2 * channels),
    )(hidden, hidden, hidden, *halo, field, expand_weight, depth_weight, weight)


def attend_body(
    mixed_ref, cot_ref, qkv_ref, out_ref, bias_ref,
    attended_ref, grad_ref, grad_qkv_ref, grad_out_ref, grad_bias_ref,
    query_ref, key_ref, value_ref, delta_ref, mixture_ref, grad_query_ref, grad_key_ref, grad_value_ref,
    bias_total,
):
    tokens, channels = mixed_ref.shape
    places = bias_ref.shape[0]
    groups = tokens // places
    head = channels // HEADS
    scale = head ** (-0.5)
    step = 256

    def prepare(i, carry):
        here = pl.ds(pl.multiple_of(i * step, step), step)
        normed, _ = normalize(mixed_ref[here, :])
        packed = dot3(normed, qkv_ref[...], NN)
        query_ref[here, :] = packed[:, :channels] * scale
        key_ref[here, :] = packed[:, channels : 2 * channels]
        value_ref[here, :] = packed[:, 2 * channels :]
        delta_ref[here, :] = dot3(cot_ref[here, :], out_ref[...], NT)
        return carry

    lax.fori_loop(0, tokens // step, prepare, 0)
    bias_total[...] = jnp.zeros_like(bias_total)

    head_of = lax.broadcasted_iota(jnp.int32, (places, channels), 1) // head

    def spread(values):
        return jnp.concatenate(
            [jnp.where(head_of == h, values, 0.0).astype(BF16) for h in range(HEADS)], axis=0
        )

    def spread_split(values):
        high, low = split(values)
        return spread(high.astype(F32)), spread(low.astype(F32))

    def gather_heads(wide):
        total = jnp.where(head_of == 0, wide[:places], 0.0)
        for h in range(1, HEADS):
            total = total + jnp.where(head_of == h, wide[h * places : (h + 1) * places], 0.0)
        return total

    def cross(a, b):
        a_high, a_low = a
        b_high, b_low = b
        return dot(
            jnp.concatenate([a_high, a_low, a_high], axis=0),
            jnp.concatenate([b_high, b_high, b_low], axis=0),
            TN,
        )

    def one_group(g, carry):
        here = pl.ds(g, places, stride=groups)
        query = spread_split(query_ref[here, :])
        delta = spread_split(delta_ref[here, :])
        key = split(key_ref[here, :])
        value = split(value_ref[here, :])
        scores = dot3(key, query, NT) + bias_ref[...]
        powers = jnp.exp(scores - jnp.max(scores, axis=0, keepdims=True))
        weights = powers * (1.0 / jnp.sum(powers, axis=0, keepdims=True))
        weights_split = split(weights)
        mixture_ref[here, :] = gather_heads(cross(weights_split, value))
        grad_weights = dot3(value, delta, NT)
        along = jnp.sum(weights * grad_weights, axis=0, keepdims=True)
        grad_scores = weights * (grad_weights - along)
        bias_total[...] += grad_scores
        grad_split = split(grad_scores)
        grad_value_ref[here, :] = dot3(weights_split, delta, NN)
        grad_key_ref[here, :] = dot3(grad_split, query, NN)
        grad_query_ref[here, :] = gather_heads(cross(grad_split, key)) * scale
        return carry

    lax.fori_loop(0, groups, one_group, 0)

    grad_qkv_ref[...] = jnp.zeros_like(grad_qkv_ref)
    grad_out_ref[...] = jnp.zeros_like(grad_out_ref)
    half = bias_total.shape[1] // 2
    grad_bias_ref[:places, :] = bias_total[:, :half]
    grad_bias_ref[places:, :] = bias_total[:, half:]

    def finish(i, carry):
        here = pl.ds(pl.multiple_of(i * step, step), step)
        mixture = split(mixture_ref[here, :])
        attended_ref[here, :] = dot3(mixture, out_ref[...], NN)
        grad_out_ref[...] += dot3(mixture, cot_ref[here, :], TN)
        normed, spread_scale = normalize(mixed_ref[here, :])
        normed_split = split(normed)
        grad_normed = jnp.zeros((step, channels), F32)
        for k, ref in enumerate((grad_query_ref, grad_key_ref, grad_value_ref)):
            lanes = slice(k * channels, (k + 1) * channels)
            grad = split(ref[here, :])
            grad_qkv_ref[:, lanes] += dot3(normed_split, grad, TN)
            grad_normed = grad_normed + dot3(grad, qkv_ref[:, lanes], NT)
        grad_ref[here, :] = normalize_back(grad_normed, normed, spread_scale)
        return carry

    lax.fori_loop(0, tokens // step, finish, 0)


def attend(mixed, cot, qkv_weight, out_weight, bias):
    tokens, channels = mixed.shape
    places = bias.shape[0]
    return call(
        attend_body,
        (),
        [pl.BlockSpec(memory_space=pltpu.VMEM)] * 5,
        [pl.BlockSpec(memory_space=pltpu.VMEM)] * 5,
        [
            shape(tokens, channels), shape(tokens, channels), shape(channels, 3 * channels),
            shape(channels, channels), shape(2 * places, bias.shape[1] // 2),
        ],
        scratch=[pltpu.VMEM((tokens, channels), F32)] * 8 + [pltpu.VMEM(bias.shape, F32)],
        flops=6 * tokens * channels * (12 * channels + 6 * places),
        bytes_accessed=16 * tokens * channels,
    )(mixed, cot, qkv_weight, out_weight, bias)


def project_back_body(back_ref, cot_ref, depth_out_ref, weight_ref, grad_mixed_ref, grad_depth_ref):
    count, cols, wide = depth_out_ref.shape
    for i in range(count):
        for k in range(cols // 8):
            here = slice(8 * k, 8 * k + 8)
            grad_mixed_ref[i, here, :] = cot_ref[i, here, :] + back_ref[0, k, i]
    grad_mixed = grad_mixed_ref[...].reshape(count * cols, -1)
    depth_out = depth_out_ref[...].reshape(count * cols, wide)
    grad = dot3(grad_mixed, weight_ref[...], NT) * gelu_slope(depth_out, gate(depth_out))
    grad_depth_ref[...] = grad.reshape(count, cols, wide)


def project_back(back, cot, depth_out, weight):
    tile_rows, tile_cols, channels = cot.shape
    wide = depth_out.shape[2]
    count = tile_rows // GRID
    return call(
        project_back_body,
        (GRID,),
        [
            rows(1, tile_cols // 8, count, 8, channels), rows(count, tile_cols, channels),
            rows(count, tile_cols, wide), whole(wide, channels),
        ],
        [rows(count, tile_cols, channels), rows(count, tile_cols, wide)],
        [shape(tile_rows, tile_cols, channels), shape(tile_rows, tile_cols, wide)],
        flops=6 * tile_rows * tile_cols * channels * wide,
        bytes_accessed=4 * tile_rows * tile_cols * (2 * wide + 3 * channels),
    )(back, cot, depth_out, weight)


def project_grad_body(grad_mixed_ref, depth_out_ref, total_ref):
    @pl.when(pl.program_id(0) == 0)
    def _():
        total_ref[...] = jnp.zeros_like(total_ref)

    total_ref[...] += dot3(grad_mixed_ref[...], gelu(depth_out_ref[...]), TN)


def project_grad(grad_mixed, depth_out):
    tokens, channels = grad_mixed.shape
    wide = depth_out.shape[1]
    step = 256
    return call(
        project_grad_body,
        (tokens // step,),
        [rows(step, channels), rows(step, wide)],
        whole(channels, wide),
        shape(channels, wide),
        flops=6 * tokens * channels * wide,
        bytes_accessed=4 * tokens * (wide + channels),
    )(grad_mixed, depth_out)


def expand_back_body(
    grad_ref, before_ref, after_ref, top, bottom, left, right, pre_ref, field_ref, grad_mixed_ref,
    expand_ref, depth_ref, grad_field_ref, grad_expand_ref, grad_depth_ref, padded, grad_pre,
):
    step = pl.program_id(0)
    last = pl.num_programs(0) - 1

    @pl.when(step == 0)
    def _():
        grad_expand_ref[...] = jnp.zeros_like(grad_expand_ref)
        grad_depth_ref[...] = jnp.zeros_like(grad_depth_ref)

    fill_padded(padded, step, last, grad_ref, before_ref, after_ref, top, bottom, left, right)
    count, cols, wide = grad_ref.shape
    for lane in range(0, wide, 128):
        lanes = slice(lane, lane + 128)
        taps = [None] * 9
        for i in range(count):
            pre = pre_ref[i, :, lanes]
            gated = gate(pre)
            hidden = pre * gated
            total = None
            for tap in range(9):
                p, q = divmod(tap, 3)
                window = padded[i + 2 - p, 9 - q : 9 - q + cols, lanes]
                term = window * depth_ref[tap : tap + 1, lanes]
                total = term if total is None else total + term
                part = jnp.sum((window * hidden).reshape(cols // 8, 8, 128), axis=0)
                taps[tap] = part if taps[tap] is None else taps[tap] + part
            grad_pre[i * cols : (i + 1) * cols, lanes] = total * gelu_slope(pre, gated)
        for tap in range(9):
            grad_depth_ref[tap : tap + 1, lanes] += jnp.sum(taps[tap], axis=0, keepdims=True)
    field = field_ref[...].reshape(count * cols, -1)
    normed, scale = normalize(field)
    grad = split(grad_pre[...])
    grad_expand_ref[...] += dot3(normed, grad, TN)
    grad_normed = dot3(grad, expand_ref[...], NT)
    grad_field = normalize_back(grad_normed, normed, scale)
    grad_field_ref[...] = grad_mixed_ref[...] + grad_field.reshape(grad_mixed_ref.shape)


def expand_back(grad_depth_out, halo, pre, field, grad_mixed, expand_weight, depth_weight):
    tile_rows, tile_cols, channels = field.shape
    wide = pre.shape[2]
    count = tile_rows // GRID
    edge = tile_rows + 2
    return call(
        expand_back_body,
        (GRID,),
        neighbours(count, tile_cols, wide, tile_rows)
        + [whole(tile_cols, wide)] * 2
        + [whole(edge, wide)] * 2
        + [
            rows(count, tile_cols, wide), rows(count, tile_cols, channels), rows(count, tile_cols, channels),
            whole(channels, wide), whole(9, wide),
        ],
        [rows(count, tile_cols, channels), whole(channels, wide), whole(16, wide)],
        [shape(tile_rows, tile_cols, channels), shape(channels, wide), shape(16, wide)],
        scratch=[
            pltpu.VMEM((count + 2, tile_cols + 16, wide), F32),
            pltpu.VMEM((count * tile_cols, wide), F32),
        ],
        flops=12 * tile_rows * tile_cols * channels * wide,
        bytes_accessed=4 * tile_rows * tile_cols * (2 * wide + 3 * channels),
    )(grad_depth_out, grad_depth_out, grad_depth_out, *halo, pre, field, grad_mixed, expand_weight, depth_weight)


def shift(values, axes, count, by):
    ends = [(i, i + 1) for i in range(count - 1)]
    return lax.ppermute(values, axes, ends if by > 0 else [(j, i) for i, j in ends])


def surround(tile, row_count, col_count):
    top = shift(tile[-1], "row", row_count, 1)
    bottom = shift(tile[0], "row", row_count, -1)

    def column(j):
        return jnp.concatenate([top[j][None], tile[:, j], bottom[j][None]], axis=0)

    left = shift(column(-1), COLS, col_count, 1)
    right = shift(column(0), COLS, col_count, -1)
    return top, bottom, left, right


def swap(blocks):
    flat = blocks.reshape((-1,) + blocks.shape[-3:])
    return lax.all_to_all(flat, PAIRS, 0, 0, tiled=True)


def reduce_all(matrices, slots, devices):
    lanes = matrices[0].shape[-1]
    buffer = jnp.stack(matrices, axis=1)
    buffer = jnp.pad(buffer, ((0, 0), (0, slots - len(matrices)), (0, 0)))
    arrived = lax.all_to_all(buffer, ALL, 0, 0, tiled=True)
    total = jnp.sum(arrived, axis=0, keepdims=True)
    spread = jnp.broadcast_to(total, (devices, slots, lanes))
    return lax.all_to_all(spread, ALL, 0, 0, tiled=True)


def on_device(
    sizes, field, expand_weight, depth_weight, project_weight, qkv_weight, out_weight, pos_bias, cotangent
):
    row_count, col_count = sizes
    tile_rows, tile_cols, channels = field.shape
    wide = expand_weight.shape[1]
    tokens = tile_rows * tile_cols
    places = GRID * GRID
    span = tile_rows // GRID
    blocks = (GRID, tile_cols // 8, span, 8, channels)

    cot_grid = swap(
        cotangent.reshape(GRID, span, tile_cols // 8, 8, channels).transpose(0, 2, 1, 3, 4)
    ).reshape(tokens, channels)
    halo = surround(field, row_count, col_count)
    pre, hidden = expand(field.reshape(tokens, channels), expand_weight)
    pre = pre.reshape(tile_rows, tile_cols, wide)
    hidden = hidden.reshape(tile_rows, tile_cols, wide)
    mixed, depth_out = project(hidden, halo, field, expand_weight, depth_weight, project_weight)
    mixed_grid = swap(mixed).reshape(tokens, channels)
    bias = pos_bias.transpose(2, 0, 1).reshape(places, HEADS * places)
    attended, grad_grid, grad_qkv, grad_out, grad_bias = attend(
        mixed_grid, cot_grid, qkv_weight, out_weight, bias
    )
    back = swap(grad_grid.reshape(blocks)).reshape(blocks)
    grad_mixed, grad_depth_out = project_back(back, cotangent, depth_out, project_weight)
    grad_halo = surround(grad_depth_out, row_count, col_count)
    grad_project = project_grad(
        grad_mixed.reshape(tokens, channels), depth_out.reshape(tokens, wide)
    )
    placed = swap(attended.reshape(blocks)).reshape(blocks)
    block_out = (mixed + placed).transpose(0, 2, 1, 3, 4).reshape(field.shape)
    grad_field, grad_expand, grad_depth = expand_back(
        grad_depth_out, grad_halo, pre, field, grad_mixed, expand_weight, depth_weight
    )

    def parts(matrix):
        return [matrix[:, k : k + channels] for k in range(0, matrix.shape[1], channels)]

    depth_rows = jnp.pad(
        jnp.concatenate(parts(grad_depth[:9]), axis=0), ((0, channels - 9 * wide // channels), (0, 0))
    )
    total = reduce_all(
        parts(grad_expand) + parts(grad_project) + parts(grad_qkv) + [grad_out, grad_bias, depth_rows],
        16,
        channels,
    )
    grad_expand = total[:, 0:4].reshape(channels, wide)
    grad_project = total[:, 4:8].transpose(1, 2, 0).reshape(wide, channels)
    grad_qkv = total[:, 8:11].reshape(channels, 3 * channels)
    grad_out = total[:, 11]
    grad_bias = total[:, 12].reshape(2, places, 2, places).transpose(0, 2, 3, 1).reshape(pos_bias.shape)
    grad_depth = total[: 9 * wide // channels, 13].reshape(4, 9, channels).transpose(1, 0, 2).reshape(9, wide)
    return (
        block_out,
        grad_field,
        grad_expand,
        grad_depth,
        grad_project,
        grad_qkv,
        grad_out,
        grad_bias,
    )


def solution(mesh):
    row_count, col_count = mesh.devices.shape
    split_mesh = Mesh(mesh.devices.reshape(row_count, col_count // 2, 2), ALL)
    tile = P("row", COLS, None)
    return jax.shard_map(
        functools.partial(on_device, (row_count, col_count)),
        mesh=split_mesh,
        in_specs=(tile, P(), P(), P(), P(), P(), P(), tile),
        out_specs=(tile, tile, P(), P(), P(), P(), P(), P()),
        check_vma=False,
    )
```

```python
import functools

import jax
import jax.numpy as jnp
from jax import lax
from jax.experimental import pallas as pl
from jax.experimental.pallas import tpu as pltpu
from jax.sharding import Mesh, PartitionSpec as P

GRID = 8
HEADS = 4
ALL = ("row", "ch", "core")
COLS = ("ch", "core")
PAIRS = ("row", "ch")
K0 = 0.7978845608028654
K1 = K0 * 0.044715
F32 = jnp.float32
BF16 = jnp.bfloat16
NN = (((1,), (0,)), ((), ()))
NT = (((1,), (1,)), ((), ()))
TN = (((0,), (0,)), ((), ()))


def split(values):
    high = values.astype(BF16)
    return high, (values - high.astype(F32)).astype(BF16)


def dot(a, b, dims):
    return lax.dot_general(a, b, dims, preferred_element_type=F32)


def dot3(a, b, dims):
    a_high, a_low = a if isinstance(a, tuple) else split(a)
    b_high, b_low = b if isinstance(b, tuple) else split(b)
    (a_axis,), (b_axis,) = dims[0]
    return dot(
        jnp.concatenate([a_high, a_low, a_high], axis=a_axis),
        jnp.concatenate([b_high, b_high, b_low], axis=b_axis),
        dims,
    )


def normalize(values):
    center = values - jnp.mean(values, axis=-1, keepdims=True)
    spread = jnp.mean(center * center, axis=-1, keepdims=True)
    scale = lax.rsqrt(spread + 1e-05)
    return center * scale, scale


def normalize_back(grad, normed, scale):
    grad_mean = jnp.mean(grad, axis=-1, keepdims=True)
    along = jnp.mean(grad * normed, axis=-1, keepdims=True)
    return scale * (grad - grad_mean - normed * along)


def gate(values):
    return 0.5 + 0.5 * jnp.tanh(values * (K0 + K1 * (values * values)))


def gelu(values):
    return values * gate(values)


def gelu_slope(values, gated):
    return gated + 2.0 * values * (gated - gated * gated) * (K0 + (3.0 * K1) * (values * values))


def call(body, grid, in_specs, out_specs, out_shape, scratch=(), flops=0, bytes_accessed=0, limit=56):
    return pl.pallas_call(
        body,
        grid=grid,
        in_specs=in_specs,
        out_specs=out_specs,
        out_shape=out_shape,
        scratch_shapes=list(scratch),
        compiler_params=pltpu.CompilerParams(vmem_limit_bytes=limit * 2**20),
        cost_estimate=pl.CostEstimate(
            flops=flops, bytes_accessed=bytes_accessed, transcendentals=0
        ),
    )


def shape(*dims):
    return jax.ShapeDtypeStruct(dims, F32)


def whole(*dims):
    return pl.BlockSpec(dims, lambda *_: (0,) * len(dims))


def rows(*dims):
    return pl.BlockSpec(dims, lambda i: (i,) + (0,) * (len(dims) - 1))


def load_row(ref, lead, cols):
    return [ref[lead + (pl.ds(k, cols // 8, stride=8),)] for k in range(8)]


def load_rows(ref, cols):
    return jnp.concatenate(
        [part for i in range(ref.shape[0]) for part in load_row(ref, (i,), cols)], axis=0
    )


def fill_row(padded, at, row, left, right):
    cols = row.shape[0]
    padded[at, 8 : 8 + cols, :] = row
    padded[at, 0:1, :] = left
    padded[at, 1:8, :] = row[cols - 8 : cols - 1]
    padded[at, 8 + cols : 15 + cols, :] = row[1:8]
    padded[at, 15 + cols : 16 + cols, :] = right


def forward_body(
    field_ref, late_ref, cot_ref, top_ref, bottom_ref, left_ref, right_ref, expand_ref, depth_ref, weight_ref,
    sent_ref, pre_ref, depth_out_ref, padded, left, right,
):
    step = pl.program_id(0)
    last = pl.num_programs(0) - 1
    count, cols, channels = field_ref.shape
    wide = expand_ref.shape[1]
    total_rows = padded.shape[0] - 2

    @pl.when(step == 0)
    def _():
        weight = split(expand_ref[...])

        def hidden(values):
            return gelu(dot3(normalize(values)[0], weight, NN))

        left[...] = hidden(left_ref[...])
        right[...] = hidden(right_ref[...])
        for at, ref in ((0, top_ref), (total_rows + 1, bottom_ref)):
            row = hidden(jnp.concatenate(load_row(ref, (), cols), axis=0))
            fill_row(padded, at, row, left[at : at + 1, :], right[at : at + 1, :])

    @pl.when(step < last)
    def _():
        normed, _ = normalize(load_rows(field_ref, cols))
        pre = dot3(normed, expand_ref[...], NN)
        pre_ref[...] = pre.reshape(count, cols, wide)
        hidden = gelu(pre)
        for i in range(count):
            at = step * count + i + 1
            row = hidden[i * cols : (i + 1) * cols]
            fill_row(padded, at, row, left[pl.ds(at, 1), :], right[pl.ds(at, 1), :])

    @pl.when(step > 0)
    def _():
        start = (step - 1) * count
        for lane in range(0, wide, 128):
            lanes = slice(lane, lane + 128)
            for i in range(count):
                total = None
                for p in range(3):
                    for q in range(3):
                        term = padded[start + i + p, 8 * q : 8 * q + cols, lanes] * depth_ref[3 * p + q : 3 * p + q + 1, lanes]
                        total = term if total is None else total + term
                depth_out_ref[i, :, lanes] = total
        activated = gelu(depth_out_ref[...].reshape(count * cols, wide))
        mixed = dot3(activated, weight_ref[...], NN) + load_rows(late_ref, cols)
        span = total_rows // GRID
        for i in range(count):
            block, inner = divmod(i, span)
            for k in range(8):
                here = i * cols + k * (cols // 8)
                sent_ref[block, pl.ds(inner * 8 + k, cols // 8, stride=2 * span * 8), :] = mixed[
                    here : here + cols // 8
                ]
            for c in range(cols // 8):
                there = (2 * c + 1) * span * 8 + inner * 8
                sent_ref[block, there : there + 8, :] = cot_ref[i, 8 * c : 8 * c + 8, :]


def forward(field, cot, halo, expand_weight, depth_weight, weight, count=8):
    tile_rows, tile_cols, channels = field.shape
    wide = expand_weight.shape[1]
    span = tile_rows // GRID
    steps = tile_rows // count
    edge = tile_rows + 2

    def early(*dims):
        return pl.BlockSpec(dims, lambda i: (jnp.minimum(i, steps - 1),) + (0,) * (len(dims) - 1))

    def late(*dims):
        return pl.BlockSpec(dims, lambda i: (jnp.maximum(i - 1, 0),) + (0,) * (len(dims) - 1))

    return call(
        forward_body,
        (steps + 1,),
        [early(count, tile_cols, channels), late(count, tile_cols, channels), late(count, tile_cols, channels)]
        + [whole(tile_cols, channels)] * 2
        + [whole(edge, channels)] * 2
        + [whole(channels, wide), whole(9, wide), whole(wide, channels)],
        [
            late(count // span, 2 * span * tile_cols, channels),
            early(count, tile_cols, wide),
            late(count, tile_cols, wide),
        ],
        [
            shape(GRID, 2 * span * tile_cols, channels),
            shape(tile_rows, tile_cols, wide),
            shape(tile_rows, tile_cols, wide),
        ],
        scratch=[
            pltpu.VMEM((edge, tile_cols + 16, wide), F32),
            pltpu.VMEM((edge, wide), F32),
            pltpu.VMEM((edge, wide), F32),
        ],
        flops=12 * tile_rows * tile_cols * channels * wide,
        bytes_accessed=4 * tile_rows * tile_cols * (2 * wide + 5 * channels),
    )(field, field, cot, *halo, expand_weight, depth_weight, weight)


def attend_body(
    came_ref, qkv_ref, out_ref, bias_ref,
    leave_ref, grad_qkv_ref, grad_out_ref, grad_bias_ref,
    packed_ref, delta_ref, mixture_ref, grad_packed_ref, bias_total,
):
    places, both, channels = came_ref.shape
    groups = both // 2
    head = channels // HEADS
    scale = head ** (-0.5)
    step = 8
    rows_in = step * groups
    together = 4

    def chunk(i, which):
        part = came_ref[pl.ds(i * step, step), which * groups : (which + 1) * groups, :]
        return part.reshape(rows_in, channels)

    def prepare(i, carry):
        here = pl.ds(pl.multiple_of(i * rows_in, rows_in), rows_in)
        normed, _ = normalize(chunk(i, 0))
        packed = dot3(normed, qkv_ref[...], NN)
        packed_ref[0, here, :] = packed[:, :channels] * scale
        packed_ref[1, here, :] = packed[:, channels : 2 * channels]
        packed_ref[2, here, :] = packed[:, 2 * channels :]
        delta_ref[here, :] = dot3(chunk(i, 1), out_ref[...], NT)
        return carry

    lax.fori_loop(0, places // step, prepare, 0)
    bias_total[...] = jnp.zeros_like(bias_total)

    head_of = lax.broadcasted_iota(jnp.int32, (places, channels), 1) // head

    def spread(values):
        return jnp.concatenate(
            [jnp.where(head_of == h, values, 0.0).astype(BF16) for h in range(HEADS)], axis=0
        )

    def spread_split(values):
        high, low = split(values)
        return spread(high.astype(F32)), spread(low.astype(F32))

    def gather_heads(wide):
        total = jnp.where(head_of == 0, wide[:places], 0.0)
        for h in range(1, HEADS):
            total = total + jnp.where(head_of == h, wide[h * places : (h + 1) * places], 0.0)
        return total

    def some_groups(i, carry):
        here = [pl.ds(i * together + k, places, stride=groups) for k in range(together)]
        query = [spread_split(packed_ref[0, h, :]) for h in here]
        delta = [spread_split(delta_ref[h, :]) for h in here]
        key = [split(packed_ref[1, h, :]) for h in here]
        value = [split(packed_ref[2, h, :]) for h in here]
        scores = [dot3(a, b, NT) + bias_ref[...] for a, b in zip(key, query)]
        grad_weights = [dot3(a, b, NT) for a, b in zip(value, delta)]
        powers = [jnp.exp(s - jnp.max(s, axis=0, keepdims=True)) for s in scores]
        weights = [p * (1.0 / jnp.sum(p, axis=0, keepdims=True)) for p in powers]
        along = [jnp.sum(w * g, axis=0, keepdims=True) for w, g in zip(weights, grad_weights)]
        grad_scores = [w * (g - a) for w, g, a in zip(weights, grad_weights, along)]
        weights = [split(w) for w in weights]
        grad_split = [split(g) for g in grad_scores]
        mixture = [gather_heads(dot3(w, v, TN)) for w, v in zip(weights, value)]
        grad_value = [dot3(w, d, NN) for w, d in zip(weights, delta)]
        grad_key = [dot3(g, q, NN) for g, q in zip(grad_split, query)]
        grad_query = [gather_heads(dot3(g, k, TN)) * scale for g, k in zip(grad_split, key)]
        for k, h in enumerate(here):
            mixture_ref[h, :] = mixture[k]
            grad_packed_ref[0, h, :] = grad_query[k]
            grad_packed_ref[1, h, :] = grad_key[k]
            grad_packed_ref[2, h, :] = grad_value[k]
        bias_total[...] += functools.reduce(jnp.add, grad_scores)
        return carry

    lax.fori_loop(0, groups // together, some_groups, 0)

    grad_qkv_ref[...] = jnp.zeros_like(grad_qkv_ref)
    grad_out_ref[...] = jnp.zeros_like(grad_out_ref)
    half = bias_total.shape[1] // 2
    grad_bias_ref[:places, :] = bias_total[:, :half]
    grad_bias_ref[places:, :] = bias_total[:, half:]

    def finish(i, carry):
        here = pl.ds(pl.multiple_of(i * rows_in, rows_in), rows_in)
        mixture = split(mixture_ref[here, :])
        normed, spread_scale = normalize(chunk(i, 0))
        grad = split(jnp.concatenate([grad_packed_ref[k, here, :] for k in range(3)], axis=1))
        grad_normed = dot3(grad, qkv_ref[...], NT)
        grad_in = normalize_back(grad_normed, normed, spread_scale)
        attended = dot3(mixture, out_ref[...], NN)
        leave_ref[pl.ds(i * step, step), :groups, :] = grad_in.reshape(step, groups, channels)
        leave_ref[pl.ds(i * step, step), groups:, :] = attended.reshape(step, groups, channels)
        grad_out_ref[...] += dot3(mixture, chunk(i, 1), TN)
        grad_qkv_ref[...] += dot3(normed, grad, TN)
        return carry

    lax.fori_loop(0, places // step, finish, 0)


def attend(came, qkv_weight, out_weight, bias):
    places, both, channels = came.shape
    tokens = places * both // 2
    return call(
        attend_body,
        (),
        [pl.BlockSpec(memory_space=pltpu.VMEM)] * 4,
        [pl.BlockSpec(memory_space=pltpu.VMEM)] * 4,
        [
            shape(places, both, channels), shape(channels, 3 * channels),
            shape(channels, channels), shape(2 * places, bias.shape[1] // 2),
        ],
        scratch=[
            pltpu.VMEM((3, tokens, channels), F32),
            pltpu.VMEM((tokens, channels), F32),
            pltpu.VMEM((tokens, channels), F32),
            pltpu.VMEM((3, tokens, channels), F32),
            pltpu.VMEM(bias.shape, F32),
        ],
        flops=6 * tokens * channels * (12 * channels + 6 * places),
        bytes_accessed=16 * tokens * channels,
    )(came, qkv_weight, out_weight, bias)


def project_back_body(
    came_ref, sent_ref, depth_out_ref, weight_ref,
    block_out_ref, grad_mixed_ref, grad_depth_ref, top_ref, bottom_ref, left_ref, right_ref, total_ref,
):
    step = pl.program_id(0)
    last = pl.num_programs(0) - 1
    count, cols, wide = depth_out_ref.shape
    span = count // came_ref.shape[0]
    piece = span * 8

    @pl.when(step == 0)
    def _():
        total_ref[...] = jnp.zeros_like(total_ref)

    parts = []
    for i in range(count):
        block, inner = divmod(i, span)
        for c in range(cols // 8):
            at = 2 * c * piece + inner * 8
            block_out_ref[i, 8 * c : 8 * c + 8, :] = (
                sent_ref[block, at : at + 8, :] + came_ref[block, at + piece : at + piece + 8, :]
            )
        for k in range(8):
            at = inner * 8 + k
            parts.append(
                came_ref[block, pl.ds(at, cols // 8, stride=2 * piece), :]
                + sent_ref[block, pl.ds(at + piece, cols // 8, stride=2 * piece), :]
            )
    grad_mixed = jnp.concatenate(parts, axis=0)
    grad_mixed_ref[...] = grad_mixed.reshape(grad_mixed_ref.shape)
    mixed_split = split(grad_mixed)
    depth_out = depth_out_ref[...].reshape(count * cols, wide)
    gated = gate(depth_out)
    grad = dot3(mixed_split, weight_ref[...], NT) * gelu_slope(depth_out, gated)
    grad_depth_ref[...] = grad.reshape(count, cols, wide)
    total_ref[...] += dot3(mixed_split, depth_out * gated, TN)
    left_ref[...] = grad_depth_ref[:, 0, :]
    right_ref[...] = grad_depth_ref[:, cols - 1, :]

    @pl.when(step == 0)
    def _():
        top_ref[...] = grad_depth_ref[0]

    @pl.when(step == last)
    def _():
        bottom_ref[...] = grad_depth_ref[count - 1]


def project_back(came, sent, depth_out, weight, count=8):
    tile_rows, tile_cols, wide = depth_out.shape
    channels = weight.shape[1]
    span = tile_rows // GRID
    tile = rows(count, tile_cols, channels)
    return call(
        project_back_body,
        (tile_rows // count,),
        [rows(count // span, 2 * span * tile_cols, channels)] * 2
        + [rows(count, tile_cols, wide), whole(wide, channels)],
        [tile, tile, rows(count, tile_cols, wide)]
        + [whole(tile_cols, wide)] * 2
        + [rows(count, wide)] * 2
        + [whole(channels, wide)],
        [shape(tile_rows, tile_cols, channels)] * 2
        + [shape(tile_rows, tile_cols, wide)]
        + [shape(tile_cols, wide)] * 2
        + [shape(tile_rows, wide)] * 2
        + [shape(channels, wide)],
        flops=12 * tile_rows * tile_cols * channels * wide,
        bytes_accessed=4 * tile_rows * tile_cols * (2 * wide + 6 * channels),
    )(came, sent, depth_out, weight)


def expand_back_body(
    grad_ref, before_ref, after_ref, top, bottom, left, right, pre_ref, field_ref, grad_mixed_ref,
    expand_ref, depth_ref, grad_field_ref, grad_expand_ref, grad_depth_ref, padded, grad_pre,
):
    step = pl.program_id(0)
    last = pl.num_programs(0) - 1
    count, cols, wide = grad_ref.shape

    @pl.when(step == 0)
    def _():
        grad_expand_ref[...] = jnp.zeros_like(grad_expand_ref)
        grad_depth_ref[...] = jnp.zeros_like(grad_depth_ref)

    def fill(at, row):
        edge = pl.ds(step * count + at, 1)
        fill_row(padded, at, row, left[edge, :], right[edge, :])

    fill(0, jnp.where(step == 0, top[...], before_ref[0]))
    fill(count + 1, jnp.where(step == last, bottom[...], after_ref[0]))
    for i in range(count):
        fill(i + 1, grad_ref[i])
    for lane in range(0, wide, 128):
        lanes = slice(lane, lane + 128)
        taps = [None] * 9
        for i in range(count):
            pre = pre_ref[i, :, lanes]
            gated = gate(pre)
            hidden = pre * gated
            total = None
            for tap in range(9):
                p, q = divmod(tap, 3)
                window = padded[i + 2 - p, 8 * (2 - q) : 8 * (2 - q) + cols, lanes]
                term = window * depth_ref[tap : tap + 1, lanes]
                total = term if total is None else total + term
                part = jnp.sum((window * hidden).reshape(cols // 8, 8, 128), axis=0)
                taps[tap] = part if taps[tap] is None else taps[tap] + part
            grad_pre[i * cols : (i + 1) * cols, lanes] = total * gelu_slope(pre, gated)
        for tap in range(9):
            grad_depth_ref[tap : tap + 1, lanes] += jnp.sum(taps[tap], axis=0, keepdims=True)
    normed, scale = normalize(load_rows(field_ref, cols))
    grad = split(grad_pre[...])
    grad_expand_ref[...] += dot3(normed, grad, TN)
    grad_normed = dot3(grad, expand_ref[...], NT)
    grad_field = normalize_back(grad_normed, normed, scale) + grad_mixed_ref[...].reshape(count * cols, -1)
    for i in range(count):
        for k in range(8):
            here = i * cols + k * (cols // 8)
            grad_field_ref[i, pl.ds(k, cols // 8, stride=8), :] = grad_field[here : here + cols // 8]


def expand_back(grad_depth_out, halo, pre, field, grad_mixed, expand_weight, depth_weight, count=8):
    tile_rows, tile_cols, channels = field.shape
    wide = pre.shape[2]
    edge = tile_rows + 2
    return call(
        expand_back_body,
        (tile_rows // count,),
        [
            rows(count, tile_cols, wide),
            pl.BlockSpec((1, tile_cols, wide), lambda i: (jnp.maximum(count * i - 1, 0), 0, 0)),
            pl.BlockSpec((1, tile_cols, wide), lambda i: (jnp.minimum(count * i + count, tile_rows - 1), 0, 0)),
        ]
        + [whole(tile_cols, wide)] * 2
        + [whole(edge, wide)] * 2
        + [
            rows(count, tile_cols, wide), rows(count, tile_cols, channels), rows(count, tile_cols, channels),
            whole(channels, wide), whole(9, wide),
        ],
        [rows(count, tile_cols, channels), whole(channels, wide), whole(16, wide)],
        [shape(tile_rows, tile_cols, channels), shape(channels, wide), shape(16, wide)],
        scratch=[
            pltpu.VMEM((count + 2, tile_cols + 16, wide), F32),
            pltpu.VMEM((count * tile_cols, wide), F32),
        ],
        flops=12 * tile_rows * tile_cols * channels * wide,
        bytes_accessed=4 * tile_rows * tile_cols * (2 * wide + 3 * channels),
    )(grad_depth_out, grad_depth_out, grad_depth_out, *halo, pre, field, grad_mixed, expand_weight, depth_weight)


SLOTS = 16


def pack_body(expand_ref, project_ref, qkv_ref, out_ref, bias_ref, depth_ref, packed_ref):
    size = out_ref.shape[0]
    slot = 0
    for ref in (expand_ref, project_ref, qkv_ref, out_ref, bias_ref):
        for lane in range(0, ref.shape[1], size):
            packed_ref[pl.ds(slot, size, stride=SLOTS), :] = ref[:, lane : lane + size]
            slot += 1
    taps = depth_ref.shape[0]
    empty = jnp.zeros((size, size), F32)
    packed_ref[pl.ds(slot, size, stride=SLOTS), :] = empty
    for k in range(depth_ref.shape[1] // size):
        packed_ref[pl.ds(slot + SLOTS * taps * k, taps, stride=SLOTS), :] = depth_ref[:, k * size : (k + 1) * size]
    for spare in range(slot + 1, SLOTS):
        packed_ref[pl.ds(spare, size, stride=SLOTS), :] = empty


def total_body(came_ref, total_ref):
    total = jnp.sum(came_ref[...], axis=0, keepdims=True)
    total_ref[...] = jnp.broadcast_to(total, total_ref.shape)


def unpack_body(packed_ref, expand_ref, project_ref, qkv_ref, out_ref, bias_ref, depth_ref):
    size = out_ref.shape[0]
    places = bias_ref.shape[1]

    def matrix(slot, count=size, first=0):
        return packed_ref[pl.ds(slot + SLOTS * first, count, stride=SLOTS), :]

    slot = 0
    for k in range(expand_ref.shape[1] // size):
        expand_ref[:, k * size : (k + 1) * size] = matrix(slot)
        slot += 1
    for k in range(project_ref.shape[0] // size):
        project_ref[k * size : (k + 1) * size, :] = matrix(slot).T
        slot += 1
    for k in range(qkv_ref.shape[1] // size):
        qkv_ref[:, k * size : (k + 1) * size] = matrix(slot)
        slot += 1
    out_ref[...] = matrix(slot)
    bias = matrix(slot + 1)
    for h in range(HEADS):
        at, lane = divmod(h, 2)
        bias_ref[h] = bias[at * places : (at + 1) * places, lane * places : (lane + 1) * places].T
    taps = 16
    for k in range(depth_ref.shape[1] // size):
        depth_ref[:, k * size : (k + 1) * size] = matrix(slot + 2, taps, taps * k)[: depth_ref.shape[0]]


def reduce_all(grads, like):
    size = grads[3].shape[0]
    vmem = pl.BlockSpec(memory_space=pltpu.VMEM)
    packed = call(pack_body, (), [vmem] * 6, vmem, shape(size * SLOTS, size))(*grads)
    came = lax.all_to_all(packed.reshape(size, SLOTS, size), ALL, 0, 0, tiled=True)
    total = call(total_body, (), [vmem], vmem, shape(size, SLOTS, size))(came)
    came = lax.all_to_all(total, ALL, 0, 0, tiled=True)
    return call(unpack_body, (), [vmem], [vmem] * 6, [shape(*a.shape) for a in like])(
        came.reshape(size * SLOTS, size)
    )


def shift(values, axes, count, by):
    ends = [(i, i + 1) for i in range(count - 1)]
    return lax.ppermute(values, axes, ends if by > 0 else [(j, i) for i, j in ends])


def surround(first, last, left, right, row_count, col_count):
    top = shift(last, "row", row_count, 1)
    bottom = shift(first, "row", row_count, -1)

    def column(edge, j):
        return jnp.concatenate([top[j : j + 1], edge, bottom[j : j + 1]], axis=0)

    end = first.shape[0] - 1
    return (
        top,
        bottom,
        shift(column(right, end), COLS, col_count, 1),
        shift(column(left, 0), COLS, col_count, -1),
    )


def swap(blocks):
    places = GRID * GRID
    flat = blocks.reshape(places, -1, blocks.shape[-1])
    return lax.all_to_all(flat, PAIRS, 0, 0, tiled=True)


def on_device(
    sizes, field, expand_weight, depth_weight, project_weight, qkv_weight, out_weight, pos_bias, cotangent
):
    places = GRID * GRID
    halo = surround(field[0], field[-1], field[:, 0], field[:, -1], *sizes)
    sent, pre, depth_out = forward(field, cotangent, halo, expand_weight, depth_weight, project_weight)
    bias = pos_bias.transpose(2, 0, 1).reshape(places, HEADS * places)
    leave, grad_qkv, grad_out, grad_bias = attend(swap(sent), qkv_weight, out_weight, bias)
    came = swap(leave).reshape(sent.shape)
    block_out, grad_mixed, grad_depth_out, *edges, grad_project = project_back(
        came, sent, depth_out, project_weight
    )
    halo = surround(*edges, *sizes)
    grad_field, grad_expand, grad_depth = expand_back(
        grad_depth_out, halo, pre, field, grad_mixed, expand_weight, depth_weight
    )
    grad_expand, grad_project, grad_qkv, grad_out, grad_bias, grad_depth = reduce_all(
        (grad_expand, grad_project, grad_qkv, grad_out, grad_bias, grad_depth),
        (expand_weight, project_weight, qkv_weight, out_weight, pos_bias, depth_weight),
    )
    return (
        block_out,
        grad_field,
        grad_expand,
        grad_depth,
        grad_project,
        grad_qkv,
        grad_out,
        grad_bias,
    )


def solution(mesh):
    row_count, col_count = mesh.devices.shape
    split_mesh = Mesh(mesh.devices.reshape(row_count, col_count // 2, 2), ALL)
    tile = P("row", COLS, None)
    return jax.shard_map(
        functools.partial(on_device, (row_count, col_count)),
        mesh=split_mesh,
        in_specs=(tile, P(), P(), P(), P(), P(), P(), tile),
        out_specs=(tile, tile, P(), P(), P(), P(), P(), P()),
        check_vma=False,
    )
```

```python
import functools

import jax
import jax.numpy as jnp
from jax import lax
from jax.experimental import pallas as pl
from jax.experimental.pallas import tpu as pltpu
from jax.sharding import Mesh, PartitionSpec as P

GRID = 8
HEADS = 4
ALL = ("row", "ch", "core")
COLS = ("ch", "core")
PAIRS = ("row", "ch")
K0 = 0.7978845608028654
K1 = K0 * 0.044715
F32 = jnp.float32
BF16 = jnp.bfloat16
NN = (((1,), (0,)), ((), ()))
NT = (((1,), (1,)), ((), ()))
TN = (((0,), (0,)), ((), ()))


def split(values):
    high = values.astype(BF16)
    return high, (values - high.astype(F32)).astype(BF16)


def dot(a, b, dims):
    return lax.dot_general(a, b, dims, preferred_element_type=F32)


def dot3(a, b, dims):
    a_high, a_low = a if isinstance(a, tuple) else split(a)
    b_high, b_low = b if isinstance(b, tuple) else split(b)
    (a_axis,), (b_axis,) = dims[0]
    return dot(
        jnp.concatenate([a_high, a_low, a_high], axis=a_axis),
        jnp.concatenate([b_high, b_high, b_low], axis=b_axis),
        dims,
    )


def normalize(values):
    center = values - jnp.mean(values, axis=-1, keepdims=True)
    spread = jnp.mean(center * center, axis=-1, keepdims=True)
    scale = lax.rsqrt(spread + 1e-05)
    return center * scale, scale


def normalize_back(grad, normed, scale):
    grad_mean = jnp.mean(grad, axis=-1, keepdims=True)
    along = jnp.mean(grad * normed, axis=-1, keepdims=True)
    return scale * (grad - grad_mean - normed * along)


def gate(values):
    return 0.5 + 0.5 * jnp.tanh(values * (K0 + K1 * (values * values)))


def gelu(values):
    return values * gate(values)


def gelu_slope(values, gated):
    return gated + 2.0 * values * (gated - gated * gated) * (K0 + (3.0 * K1) * (values * values))


def call(body, grid, in_specs, out_specs, out_shape, scratch=(), flops=0, bytes_accessed=0, limit=22):
    return pl.pallas_call(
        body,
        grid=grid,
        in_specs=in_specs,
        out_specs=out_specs,
        out_shape=out_shape,
        scratch_shapes=list(scratch),
        compiler_params=pltpu.CompilerParams(vmem_limit_bytes=limit * 2**20),
        cost_estimate=pl.CostEstimate(
            flops=flops, bytes_accessed=bytes_accessed, transcendentals=0
        ),
    )


def shape(*dims):
    return jax.ShapeDtypeStruct(dims, F32)


def whole(*dims):
    return pl.BlockSpec(dims, lambda *_: (0,) * len(dims))


def rows(*dims):
    return pl.BlockSpec(dims, lambda i: (i,) + (0,) * (len(dims) - 1))


def load_row(ref, lead, cols):
    return [ref[lead + (pl.ds(k, cols // 8, stride=8),)] for k in range(8)]


def load_rows(ref, cols):
    return jnp.concatenate(
        [part for i in range(ref.shape[0]) for part in load_row(ref, (i,), cols)], axis=0
    )


def fill_row(padded, at, row, left, right):
    cols = row.shape[0]
    padded[at, 8 : 8 + cols, :] = row
    padded[at, 0:1, :] = left
    padded[at, 1:8, :] = row[cols - 8 : cols - 1]
    padded[at, 8 + cols : 15 + cols, :] = row[1:8]
    padded[at, 15 + cols : 16 + cols, :] = right


def forward_body(
    field_ref, late_ref, top_ref, bottom_ref, left_ref, right_ref, expand_ref, depth_ref, weight_ref,
    sent_ref, pre_ref, depth_out_ref, depth_top_ref, depth_bottom_ref, depth_left_ref, depth_right_ref,
    padded, left, right,
):
    step = pl.program_id(0)
    last = pl.num_programs(0) - 1
    count, cols, channels = field_ref.shape
    wide = expand_ref.shape[1]
    total_rows = padded.shape[0] - 2

    @pl.when(step == 0)
    def _():
        weight = split(expand_ref[...])

        def hidden(values):
            return gelu(dot3(normalize(values)[0], weight, NN))

        left[...] = hidden(left_ref[...])
        right[...] = hidden(right_ref[...])
        for at, ref in ((0, top_ref), (total_rows + 1, bottom_ref)):
            row = hidden(jnp.concatenate(load_row(ref, (), cols), axis=0))
            fill_row(padded, at, row, left[at : at + 1, :], right[at : at + 1, :])

    @pl.when(step < last)
    def _():
        normed, _ = normalize(load_rows(field_ref, cols))
        pre = dot3(normed, expand_ref[...], NN)
        pre_ref[...] = pre.reshape(count, cols, wide)
        hidden = gelu(pre)
        for i in range(count):
            at = step * count + i + 1
            row = hidden[i * cols : (i + 1) * cols]
            fill_row(padded, at, row, left[pl.ds(at, 1), :], right[pl.ds(at, 1), :])

    @pl.when(step > 0)
    def _():
        start = (step - 1) * count
        for lane in range(0, wide, 128):
            lanes = slice(lane, lane + 128)
            for i in range(count):
                total = None
                for p in range(3):
                    for q in range(3):
                        term = padded[start + i + p, 8 * q : 8 * q + cols, lanes] * depth_ref[3 * p + q : 3 * p + q + 1, lanes]
                        total = term if total is None else total + term
                depth_out_ref[i, :, lanes] = total
        depth_left_ref[...] = depth_out_ref[:, 0, :]
        depth_right_ref[...] = depth_out_ref[:, cols - 1, :]
        activated = gelu(depth_out_ref[...].reshape(count * cols, wide))
        mixed = dot3(activated, weight_ref[...], NN) + load_rows(late_ref, cols)
        span = total_rows // GRID
        for i in range(count):
            block, inner = divmod(i, span)
            for k in range(8):
                here = i * cols + k * (cols // 8)
                sent_ref[block, pl.ds(inner * 8 + k, cols // 8, stride=span * 8), :] = mixed[
                    here : here + cols // 8
                ]

    @pl.when(step == 1)
    def _():
        depth_top_ref[...] = depth_out_ref[0]

    @pl.when(step == last)
    def _():
        depth_bottom_ref[...] = depth_out_ref[count - 1]


def forward(field, halo, expand_weight, depth_weight, weight, count=8):
    tile_rows, tile_cols, channels = field.shape
    wide = expand_weight.shape[1]
    span = tile_rows // GRID
    steps = tile_rows // count
    edge = tile_rows + 2

    def early(*dims):
        return pl.BlockSpec(dims, lambda i: (jnp.minimum(i, steps - 1),) + (0,) * (len(dims) - 1))

    def late(*dims):
        return pl.BlockSpec(dims, lambda i: (jnp.maximum(i - 1, 0),) + (0,) * (len(dims) - 1))

    return call(
        forward_body,
        (steps + 1,),
        [early(count, tile_cols, channels), late(count, tile_cols, channels)]
        + [whole(tile_cols, channels)] * 2
        + [whole(edge, channels)] * 2
        + [whole(channels, wide), whole(9, wide), whole(wide, channels)],
        [
            late(count // span, span * tile_cols, channels),
            early(count, tile_cols, wide),
            late(count, tile_cols, wide),
            whole(tile_cols, wide),
            whole(tile_cols, wide),
            late(count, wide),
            late(count, wide),
        ],
        [
            shape(GRID, span * tile_cols, channels),
            pltpu.HBM((tile_rows, tile_cols, wide), F32),
            pltpu.HBM((tile_rows, tile_cols, wide), F32),
            pltpu.HBM((tile_cols, wide), F32),
            pltpu.HBM((tile_cols, wide), F32),
            pltpu.HBM((tile_rows, wide), F32),
            pltpu.HBM((tile_rows, wide), F32),
        ],
        scratch=[
            pltpu.VMEM((edge, tile_cols + 16, wide), F32),
            pltpu.VMEM((edge, wide), F32),
            pltpu.VMEM((edge, wide), F32),
        ],
        flops=12 * tile_rows * tile_cols * channels * wide,
        bytes_accessed=4 * tile_rows * tile_cols * (2 * wide + 3 * channels),
    )(field, field, *halo, expand_weight, depth_weight, weight)


def arrange_body(tile_ref, sent_ref):
    tile_rows, cols, _ = tile_ref.shape
    span = tile_rows // GRID
    for i in range(tile_rows):
        block, inner = divmod(i, span)
        for c in range(cols // 8):
            there = c * span * 8 + inner * 8
            sent_ref[block, there : there + 8, :] = tile_ref[i, 8 * c : 8 * c + 8, :]


def arrange(tile):
    tile_rows, tile_cols, channels = tile.shape
    vmem = pl.BlockSpec(memory_space=pltpu.VMEM)
    return call(arrange_body, (), [vmem], vmem, shape(GRID, tile_rows * tile_cols // GRID, channels))(tile)


def attend_body(
    mixed_ref, cot_ref, qkv_ref, out_ref, bias_ref,
    leave_ref, mixture_out, grad_packed_out, grad_bias_ref,
    packed_ref, delta_ref, mixture_ref, grad_packed_ref, bias_total, done,
):
    places, groups, channels = mixed_ref.shape
    head = channels // HEADS
    scale = head ** (-0.5)
    step = 32
    rows_in = step * groups
    together = 4

    def chunk(i, ref):
        return ref[pl.ds(i * step, step)].reshape(rows_in, channels)

    def prepare(i, carry):
        here = pl.ds(pl.multiple_of(i * rows_in, rows_in), rows_in)
        normed, _ = normalize(chunk(i, mixed_ref))
        packed = dot3(normed, qkv_ref[...], NN)
        packed_ref[0, here, :] = packed[:, :channels] * scale
        packed_ref[1, here, :] = packed[:, channels : 2 * channels]
        packed_ref[2, here, :] = packed[:, 2 * channels :]
        delta_ref[here, :] = dot3(chunk(i, cot_ref), out_ref[...], NT)
        return carry

    lax.fori_loop(0, places // step, prepare, 0)
    bias_total[...] = jnp.zeros_like(bias_total)

    head_of = lax.broadcasted_iota(jnp.int32, (places, channels), 1) // head

    def spread(values):
        return jnp.concatenate(
            [jnp.where(head_of == h, values, 0.0).astype(BF16) for h in range(HEADS)], axis=0
        )

    def spread_split(values):
        high, low = split(values)
        return spread(high.astype(F32)), spread(low.astype(F32))

    def gather_heads(wide):
        total = jnp.where(head_of == 0, wide[:places], 0.0)
        for h in range(1, HEADS):
            total = total + jnp.where(head_of == h, wide[h * places : (h + 1) * places], 0.0)
        return total

    def some_groups(i, carry):
        here = [pl.ds(i * together + k, places, stride=groups) for k in range(together)]
        query = [spread_split(packed_ref[0, h, :]) for h in here]
        delta = [spread_split(delta_ref[h, :]) for h in here]
        key = [split(packed_ref[1, h, :]) for h in here]
        value = [split(packed_ref[2, h, :]) for h in here]
        scores = [dot3(a, b, NT) + bias_ref[...] for a, b in zip(key, query)]
        grad_weights = [dot3(a, b, NT) for a, b in zip(value, delta)]
        powers = [jnp.exp(s - jnp.max(s, axis=0, keepdims=True)) for s in scores]
        weights = [p * (1.0 / jnp.sum(p, axis=0, keepdims=True)) for p in powers]
        along = [jnp.sum(w * g, axis=0, keepdims=True) for w, g in zip(weights, grad_weights)]
        grad_scores = [w * (g - a) for w, g, a in zip(weights, grad_weights, along)]
        weights = [split(w) for w in weights]
        grad_split = [split(g) for g in grad_scores]
        mixture = [gather_heads(dot3(w, v, TN)) for w, v in zip(weights, value)]
        grad_value = [dot3(w, d, NN) for w, d in zip(weights, delta)]
        grad_key = [dot3(g, q, NN) for g, q in zip(grad_split, query)]
        grad_query = [gather_heads(dot3(g, k, TN)) * scale for g, k in zip(grad_split, key)]
        for k, h in enumerate(here):
            mixture_ref[h, :] = mixture[k]
            grad_packed_ref[0, h, :] = grad_query[k]
            grad_packed_ref[1, h, :] = grad_key[k]
            grad_packed_ref[2, h, :] = grad_value[k]
        bias_total[...] += functools.reduce(jnp.add, grad_scores)
        return carry

    lax.fori_loop(0, groups // together, some_groups, 0)

    copies = [
        pltpu.make_async_copy(mixture_ref, mixture_out, done.at[0]),
        pltpu.make_async_copy(grad_packed_ref, grad_packed_out, done.at[1]),
    ]
    for copy in copies:
        copy.start()
    half = bias_total.shape[1] // 2
    grad_bias_ref[:places, :] = bias_total[:, :half]
    grad_bias_ref[places:, :] = bias_total[:, half:]

    def finish(i, carry):
        here = pl.ds(pl.multiple_of(i * rows_in, rows_in), rows_in)
        normed, spread_scale = normalize(chunk(i, mixed_ref))
        grad = jnp.concatenate([grad_packed_ref[k, here, :] for k in range(3)], axis=1)
        grad_in = normalize_back(dot3(grad, qkv_ref[...], NT), normed, spread_scale)
        leave_ref[pl.ds(i * step, step)] = grad_in.reshape(step, groups, channels)
        return carry

    lax.fori_loop(0, places // step, finish, 0)
    for copy in copies:
        copy.wait()


def attend(mixed, cot, qkv_weight, out_weight, bias):
    places, groups, channels = mixed.shape
    tokens = places * groups
    vmem = pl.BlockSpec(memory_space=pltpu.VMEM)
    return call(
        attend_body,
        (),
        [vmem] * 5,
        [vmem, pl.BlockSpec(memory_space=pl.ANY), pl.BlockSpec(memory_space=pl.ANY), vmem],
        [
            shape(places, groups, channels), pltpu.HBM((tokens, channels), F32), pltpu.HBM((3, tokens, channels), F32),
            shape(2 * places, bias.shape[1] // 2),
        ],
        scratch=[
            pltpu.VMEM((3, tokens, channels), F32),
            pltpu.VMEM((tokens, channels), F32),
            pltpu.VMEM((tokens, channels), F32),
            pltpu.VMEM((3, tokens, channels), F32),
            pltpu.VMEM(bias.shape, F32),
            pltpu.SemaphoreType.DMA((2,)),
        ],
        flops=6 * tokens * channels * (12 * channels + 6 * places),
        bytes_accessed=16 * tokens * channels,
    )(mixed, cot, qkv_weight, out_weight, bias)


def attend_late_body(
    mixed_ref, cot_ref, mixture_ref, grad_packed_ref, out_ref, attended_ref, grad_qkv_ref, grad_out_ref
):
    @pl.when(pl.program_id(0) == 0)
    def _():
        grad_qkv_ref[...] = jnp.zeros_like(grad_qkv_ref)
        grad_out_ref[...] = jnp.zeros_like(grad_out_ref)

    step, groups, channels = mixed_ref.shape
    mixture = split(mixture_ref[...])
    attended_ref[...] = dot3(mixture, out_ref[...], NN).reshape(attended_ref.shape)
    grad_out_ref[...] += dot3(mixture, cot_ref[...].reshape(step * groups, channels), TN)
    normed, _ = normalize(mixed_ref[...].reshape(step * groups, channels))
    grad = jnp.concatenate([grad_packed_ref[k] for k in range(3)], axis=1)
    grad_qkv_ref[...] += dot3(normed, grad, TN)


def attend_late(mixed, cot, mixture, grad_packed, out_weight, step=16):
    places, groups, channels = mixed.shape
    tile = rows(step, groups, channels)
    return call(
        attend_late_body,
        (places // step,),
        [
            tile, tile, rows(step * groups, channels),
            pl.BlockSpec((3, step * groups, channels), lambda i: (0, i, 0)), whole(channels, channels),
        ],
        [tile, whole(channels, 3 * channels), whole(channels, channels)],
        [shape(places, groups, channels), shape(channels, 3 * channels), shape(channels, channels)],
        flops=30 * places * groups * channels * channels,
        bytes_accessed=28 * places * groups * channels,
    )(mixed, cot, mixture, grad_packed, out_weight)


def edges_body(
    came_ref, cot_ref, top_ref, bottom_ref, left_ref, right_ref, weight_ref,
    grad_top_ref, grad_bottom_ref, grad_left_ref, grad_right_ref, mixed,
):
    tile_rows, cols, _ = cot_ref.shape
    span = tile_rows // GRID
    piece = span * 8
    sides = 2 * cols
    for at, i in ((0, 0), (cols, tile_rows - 1)):
        block, inner = divmod(i, span)
        for k in range(8):
            here = at + k * (cols // 8)
            mixed[here : here + cols // 8] = (
                came_ref[block, pl.ds(inner * 8 + k, cols // 8, stride=piece), :]
                + cot_ref[i, pl.ds(k, cols // 8, stride=8), :]
            )
    for at, j in ((sides, 0), (sides + tile_rows, cols - 1)):
        first = (j // 8) * piece + j % 8
        for block in range(GRID):
            mixed[at + block * span : at + (block + 1) * span] = came_ref[block, pl.ds(first, span, stride=8), :]
        mixed[at : at + tile_rows] += cot_ref[:, j, :]
    grad = dot3(mixed[...], weight_ref[...], NT)
    at = 0
    for depth_ref, grad_ref in (
        (top_ref, grad_top_ref), (bottom_ref, grad_bottom_ref), (left_ref, grad_left_ref), (right_ref, grad_right_ref)
    ):
        depth_out = depth_ref[...]
        grad_ref[...] = grad[at : at + depth_out.shape[0]] * gelu_slope(depth_out, gate(depth_out))
        at += depth_out.shape[0]


def edges(came, cot, depth_edges, weight):
    tile_rows, tile_cols, channels = cot.shape
    wide = weight.shape[0]
    vmem = pl.BlockSpec(memory_space=pltpu.VMEM)
    return call(
        edges_body,
        (),
        [vmem] * 7,
        [vmem] * 4,
        [shape(*a.shape) for a in depth_edges],
        scratch=[pltpu.VMEM((2 * tile_cols + 2 * tile_rows, channels), F32)],
        flops=12 * (tile_cols + tile_rows) * channels * wide,
        bytes_accessed=2**21,
    )(came, cot, *depth_edges, weight)


def project_back_body(
    came_ref, cot_ref, depth_out_ref, weight_ref,
    grad_mixed_ref, grad_depth_ref, total_ref,
):
    step = pl.program_id(0)
    count, cols, wide = depth_out_ref.shape
    span = count // came_ref.shape[0]
    piece = span * 8

    @pl.when(step == 0)
    def _():
        total_ref[...] = jnp.zeros_like(total_ref)

    parts = []
    for i in range(count):
        block, inner = divmod(i, span)
        for k, cot in enumerate(load_row(cot_ref, (i,), cols)):
            parts.append(came_ref[block, pl.ds(inner * 8 + k, cols // 8, stride=piece), :] + cot)
    grad_mixed = jnp.concatenate(parts, axis=0)
    grad_mixed_ref[...] = grad_mixed.reshape(grad_mixed_ref.shape)
    mixed_split = split(grad_mixed)
    depth_out = depth_out_ref[...].reshape(count * cols, wide)
    gated = gate(depth_out)
    grad = dot3(mixed_split, weight_ref[...], NT) * gelu_slope(depth_out, gated)
    grad_depth_ref[...] = grad.reshape(count, cols, wide)
    total_ref[...] += dot3(mixed_split, depth_out * gated, TN)


def project_back(came, cot, depth_out, weight, count=8):
    tile_rows, tile_cols, wide = depth_out.shape
    channels = weight.shape[1]
    span = tile_rows // GRID
    tile = rows(count, tile_cols, channels)
    return call(
        project_back_body,
        (tile_rows // count,),
        [rows(count // span, span * tile_cols, channels), tile, rows(count, tile_cols, wide), whole(wide, channels)],
        [tile, rows(count, tile_cols, wide), whole(channels, wide)],
        [shape(tile_rows, tile_cols, channels), shape(tile_rows, tile_cols, wide), shape(channels, wide)],
        flops=12 * tile_rows * tile_cols * channels * wide,
        bytes_accessed=4 * tile_rows * tile_cols * (2 * wide + 3 * channels),
        limit=56,
    )(came, cot, depth_out, weight)


def expand_back_body(
    grad_ref, before_ref, after_ref, top, bottom, left, right, pre_ref, field_ref, depth_ref,
    grad_pre_ref, grad_expand_ref, grad_depth_ref, padded,
):
    step = pl.program_id(0)
    last = pl.num_programs(0) - 1
    count, cols, wide = grad_ref.shape

    @pl.when(step == 0)
    def _():
        grad_expand_ref[...] = jnp.zeros_like(grad_expand_ref)
        grad_depth_ref[...] = jnp.zeros_like(grad_depth_ref)

    def fill(at, row):
        edge = pl.ds(step * count + at, 1)
        fill_row(padded, at, row, left[edge, :], right[edge, :])

    fill(0, jnp.where(step == 0, top[...], before_ref[0]))
    fill(count + 1, jnp.where(step == last, bottom[...], after_ref[0]))
    for i in range(count):
        fill(i + 1, grad_ref[i])
    for lane in range(0, wide, 128):
        lanes = slice(lane, lane + 128)
        taps = [None] * 9
        for i in range(count):
            pre = pre_ref[i, :, lanes]
            gated = gate(pre)
            hidden = pre * gated
            total = None
            for tap in range(9):
                p, q = divmod(tap, 3)
                window = padded[i + 2 - p, 8 * (2 - q) : 8 * (2 - q) + cols, lanes]
                term = window * depth_ref[tap : tap + 1, lanes]
                total = term if total is None else total + term
                part = jnp.sum((window * hidden).reshape(cols // 8, 8, 128), axis=0)
                taps[tap] = part if taps[tap] is None else taps[tap] + part
            grad_pre_ref[i, :, lanes] = total * gelu_slope(pre, gated)
        for tap in range(9):
            grad_depth_ref[tap : tap + 1, lanes] += jnp.sum(taps[tap], axis=0, keepdims=True)
    normed, _ = normalize(load_rows(field_ref, cols))
    grad_expand_ref[...] += dot3(normed, grad_pre_ref[...].reshape(count * cols, wide), TN)


def expand_back(grad_depth_out, halo, pre, field, depth_weight, count=8):
    tile_rows, tile_cols, channels = field.shape
    wide = pre.shape[2]
    edge = tile_rows + 2
    return call(
        expand_back_body,
        (tile_rows // count,),
        [
            rows(count, tile_cols, wide),
            pl.BlockSpec((1, tile_cols, wide), lambda i: (jnp.maximum(count * i - 1, 0), 0, 0)),
            pl.BlockSpec((1, tile_cols, wide), lambda i: (jnp.minimum(count * i + count, tile_rows - 1), 0, 0)),
        ]
        + [whole(tile_cols, wide)] * 2
        + [whole(edge, wide)] * 2
        + [rows(count, tile_cols, wide), rows(count, tile_cols, channels), whole(9, wide)],
        [rows(count, tile_cols, wide), whole(channels, wide), whole(16, wide)],
        [shape(tile_rows, tile_cols, wide), shape(channels, wide), shape(16, wide)],
        scratch=[pltpu.VMEM((count + 2, tile_cols + 16, wide), F32)],
        flops=6 * tile_rows * tile_cols * channels * wide,
        bytes_accessed=4 * tile_rows * tile_cols * (3 * wide + channels),
        limit=56,
    )(grad_depth_out, grad_depth_out, grad_depth_out, *halo, pre, field, depth_weight)


def finish_body(
    grad_pre_ref, field_ref, grad_mixed_ref, sent_ref, placed_ref, expand_ref, block_out_ref, grad_field_ref
):
    count, cols, wide = grad_pre_ref.shape
    span = count // sent_ref.shape[0]
    for i in range(count):
        block, inner = divmod(i, span)
        for c in range(cols // 8):
            there = slice(c * span * 8 + inner * 8, c * span * 8 + inner * 8 + 8)
            block_out_ref[i, 8 * c : 8 * c + 8, :] = sent_ref[block, there, :] + placed_ref[block, there, :]
    normed, scale = normalize(load_rows(field_ref, cols))
    grad_normed = dot3(grad_pre_ref[...].reshape(count * cols, wide), expand_ref[...], NT)
    grad_field = normalize_back(grad_normed, normed, scale) + grad_mixed_ref[...].reshape(count * cols, -1)
    for i in range(count):
        for k in range(8):
            here = i * cols + k * (cols // 8)
            grad_field_ref[i, pl.ds(k, cols // 8, stride=8), :] = grad_field[here : here + cols // 8]


def finish(grad_pre, field, grad_mixed, sent, placed, expand_weight, count=8):
    tile_rows, tile_cols, channels = field.shape
    wide = grad_pre.shape[2]
    span = tile_rows // GRID
    tile = rows(count, tile_cols, channels)
    blocks = rows(count // span, span * tile_cols, channels)
    return call(
        finish_body,
        (tile_rows // count,),
        [rows(count, tile_cols, wide), tile, tile, blocks, blocks, whole(channels, wide)],
        [tile, tile],
        [shape(*field.shape)] * 2,
        flops=6 * tile_rows * tile_cols * channels * wide,
        bytes_accessed=4 * tile_rows * tile_cols * (wide + 6 * channels),
        limit=56,
    )(grad_pre, field, grad_mixed, sent, placed, expand_weight)


SLOTS = 16


def pack_body(expand_ref, project_ref, qkv_ref, out_ref, bias_ref, depth_ref, packed_ref):
    size = out_ref.shape[0]
    slot = 0
    for ref in (expand_ref, project_ref, qkv_ref, out_ref, bias_ref):
        for lane in range(0, ref.shape[1], size):
            packed_ref[pl.ds(slot, size, stride=SLOTS), :] = ref[:, lane : lane + size]
            slot += 1
    taps = depth_ref.shape[0]
    empty = jnp.zeros((size, size), F32)
    packed_ref[pl.ds(slot, size, stride=SLOTS), :] = empty
    for k in range(depth_ref.shape[1] // size):
        packed_ref[pl.ds(slot + SLOTS * taps * k, taps, stride=SLOTS), :] = depth_ref[:, k * size : (k + 1) * size]
    for spare in range(slot + 1, SLOTS):
        packed_ref[pl.ds(spare, size, stride=SLOTS), :] = empty


def total_body(came_ref, total_ref):
    total = jnp.sum(came_ref[...], axis=0, keepdims=True)
    total_ref[...] = jnp.broadcast_to(total, total_ref.shape)


def unpack_body(packed_ref, expand_ref, project_ref, qkv_ref, out_ref, bias_ref, depth_ref):
    size = out_ref.shape[0]
    places = bias_ref.shape[1]

    def matrix(slot, count=size, first=0):
        return packed_ref[pl.ds(slot + SLOTS * first, count, stride=SLOTS), :]

    slot = 0
    for k in range(expand_ref.shape[1] // size):
        expand_ref[:, k * size : (k + 1) * size] = matrix(slot)
        slot += 1
    for k in range(project_ref.shape[0] // size):
        project_ref[k * size : (k + 1) * size, :] = matrix(slot).T
        slot += 1
    for k in range(qkv_ref.shape[1] // size):
        qkv_ref[:, k * size : (k + 1) * size] = matrix(slot)
        slot += 1
    out_ref[...] = matrix(slot)
    bias = matrix(slot + 1)
    for h in range(HEADS):
        at, lane = divmod(h, 2)
        bias_ref[h] = bias[at * places : (at + 1) * places, lane * places : (lane + 1) * places].T
    taps = 16
    for k in range(depth_ref.shape[1] // size):
        depth_ref[:, k * size : (k + 1) * size] = matrix(slot + 2, taps, taps * k)[: depth_ref.shape[0]]


def reduce_all(grads, like, after):
    size = grads[3].shape[0]
    vmem = pl.BlockSpec(memory_space=pltpu.VMEM)
    packed = call(pack_body, (), [vmem] * 6, vmem, shape(size * SLOTS, size))(*grads)
    packed, after = lax.optimization_barrier((packed, after))
    came = lax.all_to_all(packed.reshape(size, SLOTS, size), ALL, 0, 0, tiled=True)
    total = call(total_body, (), [vmem], vmem, shape(size, SLOTS, size))(came)
    came = lax.all_to_all(total, ALL, 0, 0, tiled=True)
    totals = call(unpack_body, (), [vmem], [vmem] * 6, [shape(*a.shape) for a in like])(
        came.reshape(size * SLOTS, size)
    )
    return totals, after


def shift(values, axes, count, by):
    ends = [(i, i + 1) for i in range(count - 1)]
    return lax.ppermute(values, axes, ends if by > 0 else [(j, i) for i, j in ends])


def beyond_rows(first, last, row_count):
    return shift(last, "row", row_count, 1), shift(first, "row", row_count, -1)


def beyond_columns(top, bottom, left, right, col_count):
    def column(edge, j):
        return jnp.concatenate([top[j : j + 1], edge, bottom[j : j + 1]], axis=0)

    end = top.shape[0] - 1
    return shift(column(right, end), COLS, col_count, 1), shift(column(left, 0), COLS, col_count, -1)


def swap(blocks):
    places = GRID * GRID
    flat = blocks.reshape(places, -1, blocks.shape[-1])
    return lax.all_to_all(flat, PAIRS, 0, 0, tiled=True)


def on_device(
    sizes, field, expand_weight, depth_weight, project_weight, qkv_weight, out_weight, pos_bias, cotangent
):
    places = GRID * GRID
    row_count, col_count = sizes
    halo = beyond_rows(field[0], field[-1], row_count)
    halo += beyond_columns(*halo, field[:, 0], field[:, -1], col_count)
    arranged, halo = lax.optimization_barrier((arrange(cotangent), halo))
    cot_grid = swap(arranged)
    sent, pre, depth_out, *depth_edges = forward(field, halo, expand_weight, depth_weight, project_weight)
    mixed_grid = swap(sent)
    bias = pos_bias.transpose(2, 0, 1).reshape(places, HEADS * places)
    leave, mixture, grad_packed, grad_bias = attend(mixed_grid, cot_grid, qkv_weight, out_weight, bias)
    came = swap(leave)
    attended, grad_qkv, grad_out = attend_late(mixed_grid, cot_grid, mixture, grad_packed, out_weight)
    came, attended = lax.optimization_barrier((came, attended))
    came = came.reshape(sent.shape)
    placed = swap(attended).reshape(sent.shape)
    first, last, left, right = edges(came, cotangent, depth_edges, project_weight)
    halo = beyond_rows(first, last, row_count)
    grad_mixed, grad_depth_out, grad_project = project_back(came, cotangent, depth_out, project_weight)
    halo, grad_depth_out = lax.optimization_barrier((halo, grad_depth_out))
    halo += beyond_columns(*halo, left, right, col_count)
    grad_pre, grad_expand, grad_depth = expand_back(grad_depth_out, halo, pre, field, depth_weight)
    totals, placed = reduce_all(
        (grad_expand, grad_project, grad_qkv, grad_out, grad_bias, grad_depth),
        (expand_weight, project_weight, qkv_weight, out_weight, pos_bias, depth_weight),
        placed,
    )
    grad_expand, grad_project, grad_qkv, grad_out, grad_bias, grad_depth = totals
    block_out, grad_field = finish(grad_pre, field, grad_mixed, sent, placed, expand_weight)
    return (
        block_out,
        grad_field,
        grad_expand,
        grad_depth,
        grad_project,
        grad_qkv,
        grad_out,
        grad_bias,
    )


def solution(mesh):
    row_count, col_count = mesh.devices.shape
    split_mesh = Mesh(mesh.devices.reshape(row_count, col_count // 2, 2), ALL)
    tile = P("row", COLS, None)
    return jax.shard_map(
        functools.partial(on_device, (row_count, col_count)),
        mesh=split_mesh,
        in_specs=(tile, P(), P(), P(), P(), P(), P(), tile),
        out_specs=(tile, tile, P(), P(), P(), P(), P(), P()),
        check_vma=False,
    )
```

```python
import functools

import jax
import jax.numpy as jnp
from jax import lax
from jax.experimental import pallas as pl
from jax.experimental.pallas import tpu as pltpu
from jax.sharding import Mesh, PartitionSpec as P

GRID = 8
HEADS = 4
ALL = ("row", "ch", "core")
COLS = ("ch", "core")
PAIRS = ("row", "ch")
K0 = 0.7978845608028654
K1 = K0 * 0.044715
F32 = jnp.float32
BF16 = jnp.bfloat16
NN = (((1,), (0,)), ((), ()))
NT = (((1,), (1,)), ((), ()))
TN = (((0,), (0,)), ((), ()))


def split(values):
    high = values.astype(BF16)
    return high, (values - high.astype(F32)).astype(BF16)


def dot(a, b, dims):
    return lax.dot_general(a, b, dims, preferred_element_type=F32)


def dot3(a, b, dims):
    a_high, a_low = a if isinstance(a, tuple) else split(a)
    b_high, b_low = b if isinstance(b, tuple) else split(b)
    (a_axis,), (b_axis,) = dims[0]
    return dot(
        jnp.concatenate([a_high, a_low, a_high], axis=a_axis),
        jnp.concatenate([b_high, b_high, b_low], axis=b_axis),
        dims,
    )


def normalize(values):
    center = values - jnp.mean(values, axis=-1, keepdims=True)
    spread = jnp.mean(center * center, axis=-1, keepdims=True)
    scale = lax.rsqrt(spread + 1e-05)
    return center * scale, scale


def normalize_back(grad, normed, scale):
    grad_mean = jnp.mean(grad, axis=-1, keepdims=True)
    along = jnp.mean(grad * normed, axis=-1, keepdims=True)
    return scale * (grad - grad_mean - normed * along)


def gate(values):
    return 0.5 + 0.5 * jnp.tanh(values * (K0 + K1 * (values * values)))


def gelu(values):
    return values * gate(values)


def gelu_slope(values, gated):
    return gated + 2.0 * values * (gated - gated * gated) * (K0 + (3.0 * K1) * (values * values))


def call(body, grid, in_specs, out_specs, out_shape, scratch=(), flops=0, bytes_accessed=0, limit=22):
    return pl.pallas_call(
        body,
        grid=grid,
        in_specs=in_specs,
        out_specs=out_specs,
        out_shape=out_shape,
        scratch_shapes=list(scratch),
        compiler_params=pltpu.CompilerParams(vmem_limit_bytes=limit * 2**20),
        cost_estimate=pl.CostEstimate(
            flops=flops, bytes_accessed=bytes_accessed, transcendentals=0
        ),
    )


def shape(*dims):
    return jax.ShapeDtypeStruct(dims, F32)


def whole(*dims):
    return pl.BlockSpec(dims, lambda *_: (0,) * len(dims))


def rows(*dims):
    return pl.BlockSpec(dims, lambda i: (i,) + (0,) * (len(dims) - 1))


def load_row(ref, lead, cols):
    return [ref[lead + (pl.ds(k, cols // 8, stride=8),)] for k in range(8)]


def load_rows(ref, cols):
    return jnp.concatenate(
        [part for i in range(ref.shape[0]) for part in load_row(ref, (i,), cols)], axis=0
    )


def fill_row(padded, at, row, left, right):
    cols = row.shape[0]
    padded[at, 8 : 8 + cols, :] = row
    padded[at, 0:1, :] = left
    padded[at, 1:8, :] = row[cols - 8 : cols - 1]
    padded[at, 8 + cols : 15 + cols, :] = row[1:8]
    padded[at, 15 + cols : 16 + cols, :] = right


def keep_row(values, flag):
    return jnp.where(flag > 0, values, 0.0)


def keep_column(values, flag, above, below):
    at = lax.broadcasted_iota(jnp.int32, values.shape, 0)
    kept = jnp.where(at == 0, above, jnp.where(at == values.shape[0] - 1, below, 1)) * flag
    return jnp.where(kept > 0, values, 0.0)


def forward_body(
    inside_ref, field_ref, late_ref, top_ref, bottom_ref, left_ref, right_ref, expand_ref, depth_ref, weight_ref,
    sent_ref, pre_ref, depth_out_ref, depth_top_ref, depth_bottom_ref, depth_left_ref, depth_right_ref,
    padded, left, right,
):
    step = pl.program_id(0)
    last = pl.num_programs(0) - 1
    count, cols, channels = field_ref.shape
    wide = expand_ref.shape[1]
    total_rows = padded.shape[0] - 2

    @pl.when(step == 0)
    def _():
        weight = split(expand_ref[...])

        def hidden(values):
            return gelu(dot3(normalize(values)[0], weight, NN))

        above, below = inside_ref[0], inside_ref[1]
        left[...] = hidden(keep_column(left_ref[...], inside_ref[2], above, below))
        right[...] = hidden(keep_column(right_ref[...], inside_ref[3], above, below))
        for at, ref, flag in ((0, top_ref, above), (total_rows + 1, bottom_ref, below)):
            row = hidden(keep_row(jnp.concatenate(load_row(ref, (), cols), axis=0), flag))
            fill_row(padded, at, row, left[at : at + 1, :], right[at : at + 1, :])

    @pl.when(step < last)
    def _():
        normed, _ = normalize(load_rows(field_ref, cols))
        pre = dot3(normed, expand_ref[...], NN)
        pre_ref[...] = pre.reshape(count, cols, wide)
        hidden = gelu(pre)
        for i in range(count):
            at = step * count + i + 1
            row = hidden[i * cols : (i + 1) * cols]
            fill_row(padded, at, row, left[pl.ds(at, 1), :], right[pl.ds(at, 1), :])

    @pl.when(step > 0)
    def _():
        start = (step - 1) * count
        for lane in range(0, wide, 128):
            lanes = slice(lane, lane + 128)
            for i in range(count):
                total = None
                for p in range(3):
                    for q in range(3):
                        term = padded[start + i + p, 8 * q : 8 * q + cols, lanes] * depth_ref[3 * p + q : 3 * p + q + 1, lanes]
                        total = term if total is None else total + term
                depth_out_ref[i, :, lanes] = total
        depth_left_ref[...] = depth_out_ref[:, 0, :]
        depth_right_ref[...] = depth_out_ref[:, cols - 1, :]
        activated = gelu(depth_out_ref[...].reshape(count * cols, wide))
        mixed = dot3(activated, weight_ref[...], NN) + load_rows(late_ref, cols)
        span = total_rows // GRID
        for i in range(count):
            block, inner = divmod(i, span)
            for k in range(8):
                here = i * cols + k * (cols // 8)
                sent_ref[block, pl.ds(inner * 8 + k, cols // 8, stride=span * 8), :] = mixed[
                    here : here + cols // 8
                ]

    @pl.when(step == 1)
    def _():
        depth_top_ref[...] = depth_out_ref[0]

    @pl.when(step == last)
    def _():
        depth_bottom_ref[...] = depth_out_ref[count - 1]


def forward(flags, field, halo, expand_weight, depth_weight, weight, count=8):
    tile_rows, tile_cols, channels = field.shape
    wide = expand_weight.shape[1]
    span = tile_rows // GRID
    steps = tile_rows // count
    edge = tile_rows + 2

    def early(*dims):
        return pl.BlockSpec(dims, lambda i: (jnp.minimum(i, steps - 1),) + (0,) * (len(dims) - 1))

    def late(*dims):
        return pl.BlockSpec(dims, lambda i: (jnp.maximum(i - 1, 0),) + (0,) * (len(dims) - 1))

    return call(
        forward_body,
        (steps + 1,),
        [pl.BlockSpec(memory_space=pltpu.SMEM), early(count, tile_cols, channels), late(count, tile_cols, channels)]
        + [whole(tile_cols, channels)] * 2
        + [whole(edge, channels)] * 2
        + [whole(channels, wide), whole(9, wide), whole(wide, channels)],
        [
            late(count // span, span * tile_cols, channels),
            early(count, tile_cols, wide),
            late(count, tile_cols, wide),
            whole(tile_cols, wide),
            whole(tile_cols, wide),
            late(count, wide),
            late(count, wide),
        ],
        [
            shape(GRID, span * tile_cols, channels),
            pltpu.HBM((tile_rows, tile_cols, wide), F32),
            pltpu.HBM((tile_rows, tile_cols, wide), F32),
            pltpu.HBM((tile_cols, wide), F32),
            pltpu.HBM((tile_cols, wide), F32),
            pltpu.HBM((tile_rows, wide), F32),
            pltpu.HBM((tile_rows, wide), F32),
        ],
        scratch=[
            pltpu.VMEM((edge, tile_cols + 16, wide), F32),
            pltpu.VMEM((edge, wide), F32),
            pltpu.VMEM((edge, wide), F32),
        ],
        flops=12 * tile_rows * tile_cols * channels * wide,
        bytes_accessed=4 * tile_rows * tile_cols * (2 * wide + 3 * channels),
    )(flags, field, field, *halo, expand_weight, depth_weight, weight)


def arrange_body(tile_ref, sent_ref):
    tile_rows, cols, _ = tile_ref.shape
    span = tile_rows // GRID
    for i in range(tile_rows):
        block, inner = divmod(i, span)
        for c in range(cols // 8):
            there = c * span * 8 + inner * 8
            sent_ref[block, there : there + 8, :] = tile_ref[i, 8 * c : 8 * c + 8, :]


def arrange(tile):
    tile_rows, tile_cols, channels = tile.shape
    vmem = pl.BlockSpec(memory_space=pltpu.VMEM)
    return call(arrange_body, (), [vmem], vmem, shape(GRID, tile_rows * tile_cols // GRID, channels))(tile)


SPARE = 8


def pitched(ref, lead, first, count, pitch, groups):
    return jnp.concatenate(
        [ref[lead + (pl.ds(pl.multiple_of((first + j) * pitch, 8), groups),)] for j in range(count)], axis=0
    )


def attend_body(
    mixed_ref, cot_ref, qkv_ref, out_ref, bias_ref,
    leave_ref, mixture_out, grad_packed_out, grad_bias_out,
    packed_ref, delta_ref, mixture_ref, grad_packed_ref, bias_total, grad_bias_ref, done,
):
    places, groups, channels = mixed_ref.shape
    head = channels // HEADS
    scale = head ** (-0.5)
    pitch = groups + SPARE
    step = 32
    rows_in = step * groups
    together = 4

    def chunk(i, ref):
        return ref[pl.ds(i * step, step)].reshape(rows_in, channels)

    def prepare(i, carry):
        normed, _ = normalize(chunk(i, mixed_ref))
        packed = dot3(normed, qkv_ref[...], NN)
        delta = dot3(chunk(i, cot_ref), out_ref[...], NT)
        for j in range(step):
            here = pl.ds(pl.multiple_of((i * step + j) * pitch, 8), groups)
            part = slice(j * groups, (j + 1) * groups)
            packed_ref[0, here, :] = packed[part, :channels] * scale
            packed_ref[1, here, :] = packed[part, channels : 2 * channels]
            packed_ref[2, here, :] = packed[part, 2 * channels :]
            delta_ref[here, :] = delta[part]
        return carry

    lax.fori_loop(0, places // step, prepare, 0)
    bias_total[...] = jnp.zeros_like(bias_total)

    head_of = lax.broadcasted_iota(jnp.int32, (places, channels), 1) // head

    def spread(values):
        return jnp.concatenate(
            [jnp.where(head_of == h, values, 0.0).astype(BF16) for h in range(HEADS)], axis=0
        )

    def spread_split(values):
        high, low = split(values)
        return spread(high.astype(F32)), spread(low.astype(F32))

    def gather_heads(wide):
        total = jnp.where(head_of == 0, wide[:places], 0.0)
        for h in range(1, HEADS):
            total = total + jnp.where(head_of == h, wide[h * places : (h + 1) * places], 0.0)
        return total

    def some_groups(i, carry):
        here = [pl.ds(i * together + k, places, stride=pitch) for k in range(together)]
        query = [spread_split(packed_ref[0, h, :]) for h in here]
        delta = [spread_split(delta_ref[h, :]) for h in here]
        key = [split(packed_ref[1, h, :]) for h in here]
        value = [split(packed_ref[2, h, :]) for h in here]
        scores = [dot3(a, b, NT) + bias_ref[...] for a, b in zip(key, query)]
        grad_weights = [dot3(a, b, NT) for a, b in zip(value, delta)]
        powers = [jnp.exp(s - jnp.max(s, axis=0, keepdims=True)) for s in scores]
        weights = [p * (1.0 / jnp.sum(p, axis=0, keepdims=True)) for p in powers]
        along = [jnp.sum(w * g, axis=0, keepdims=True) for w, g in zip(weights, grad_weights)]
        grad_scores = [w * (g - a) for w, g, a in zip(weights, grad_weights, along)]
        weights = [split(w) for w in weights]
        grad_split = [split(g) for g in grad_scores]
        mixture = [gather_heads(dot3(w, v, TN)) for w, v in zip(weights, value)]
        grad_value = [dot3(w, d, NN) for w, d in zip(weights, delta)]
        grad_key = [dot3(g, q, NN) for g, q in zip(grad_split, query)]
        grad_query = [gather_heads(dot3(g, k, TN)) * scale for g, k in zip(grad_split, key)]
        for k, h in enumerate(here):
            mixture_ref[h, :] = mixture[k]
            grad_packed_ref[0, h, :] = grad_query[k]
            grad_packed_ref[1, h, :] = grad_key[k]
            grad_packed_ref[2, h, :] = grad_value[k]
        bias_total[...] += functools.reduce(jnp.add, grad_scores)
        return carry

    lax.fori_loop(0, groups // together, some_groups, 0)

    half = bias_total.shape[1] // 2
    grad_bias_ref[:places, :] = bias_total[:, :half]
    grad_bias_ref[places:, :] = bias_total[:, half:]
    copies = [
        pltpu.make_async_copy(mixture_ref, mixture_out, done.at[0]),
        pltpu.make_async_copy(grad_packed_ref, grad_packed_out, done.at[1]),
        pltpu.make_async_copy(grad_bias_ref, grad_bias_out, done.at[2]),
    ]
    for copy in copies:
        copy.start()

    def finish(i, carry):
        normed, spread_scale = normalize(chunk(i, mixed_ref))
        grad = jnp.concatenate(
            [pitched(grad_packed_ref, (k,), i * step, step, pitch, groups) for k in range(3)], axis=1
        )
        grad_in = normalize_back(dot3(grad, qkv_ref[...], NT), normed, spread_scale)
        leave_ref[pl.ds(i * step, step)] = grad_in.reshape(step, groups, channels)
        return carry

    lax.fori_loop(0, places // step, finish, 0)
    for copy in copies:
        copy.wait()


def attend(mixed, cot, qkv_weight, out_weight, bias):
    places, groups, channels = mixed.shape
    tokens = places * groups
    padded = places * (groups + SPARE)
    vmem = pl.BlockSpec(memory_space=pltpu.VMEM)
    return call(
        attend_body,
        (),
        [vmem] * 5,
        [vmem] + [pl.BlockSpec(memory_space=pl.ANY)] * 3,
        [
            shape(places, groups, channels), pltpu.HBM((padded, channels), F32), pltpu.HBM((3, padded, channels), F32),
            pltpu.HBM((2 * places, bias.shape[1] // 2), F32),
        ],
        scratch=[
            pltpu.VMEM((3, padded, channels), F32),
            pltpu.VMEM((padded, channels), F32),
            pltpu.VMEM((padded, channels), F32),
            pltpu.VMEM((3, padded, channels), F32),
            pltpu.VMEM(bias.shape, F32),
            pltpu.VMEM((2 * places, bias.shape[1] // 2), F32),
            pltpu.SemaphoreType.DMA((3,)),
        ],
        flops=6 * tokens * channels * (12 * channels + 6 * places),
        bytes_accessed=16 * tokens * channels,
    )(mixed, cot, qkv_weight, out_weight, bias)


def attend_late_body(
    mixed_ref, cot_ref, mixture_ref, grad_packed_ref, out_ref, attended_ref, grad_qkv_ref, grad_out_ref
):
    @pl.when(pl.program_id(0) == 0)
    def _():
        grad_qkv_ref[...] = jnp.zeros_like(grad_qkv_ref)
        grad_out_ref[...] = jnp.zeros_like(grad_out_ref)

    step, groups, channels = mixed_ref.shape
    pitch = groups + SPARE
    mixture = split(pitched(mixture_ref, (), 0, step, pitch, groups))
    attended_ref[...] = dot3(mixture, out_ref[...], NN).reshape(attended_ref.shape)
    grad_out_ref[...] += dot3(mixture, cot_ref[...].reshape(step * groups, channels), TN)
    normed, _ = normalize(mixed_ref[...].reshape(step * groups, channels))
    grad = jnp.concatenate(
        [pitched(grad_packed_ref, (k,), 0, step, pitch, groups) for k in range(3)], axis=1
    )
    grad_qkv_ref[...] += dot3(normed, grad, TN)


def attend_late(mixed, cot, mixture, grad_packed, out_weight, step=16):
    places, groups, channels = mixed.shape
    tile = rows(step, groups, channels)
    return call(
        attend_late_body,
        (places // step,),
        [
            tile, tile, rows(step * (groups + SPARE), channels),
            pl.BlockSpec((3, step * (groups + SPARE), channels), lambda i: (0, i, 0)), whole(channels, channels),
        ],
        [tile, whole(channels, 3 * channels), whole(channels, channels)],
        [shape(places, groups, channels), shape(channels, 3 * channels), shape(channels, channels)],
        flops=30 * places * groups * channels * channels,
        bytes_accessed=28 * places * groups * channels,
    )(mixed, cot, mixture, grad_packed, out_weight)


def edges_body(
    came_ref, cot_ref, top_ref, bottom_ref, left_ref, right_ref, weight_ref,
    grad_top_ref, grad_bottom_ref, grad_left_ref, grad_right_ref, mixed,
):
    tile_rows, cols, _ = cot_ref.shape
    span = tile_rows // GRID
    piece = span * 8
    sides = 2 * cols
    for at, i in ((0, 0), (cols, tile_rows - 1)):
        block, inner = divmod(i, span)
        for k in range(8):
            here = at + k * (cols // 8)
            mixed[here : here + cols // 8] = (
                came_ref[block, pl.ds(inner * 8 + k, cols // 8, stride=piece), :]
                + cot_ref[i, pl.ds(k, cols // 8, stride=8), :]
            )
    for at, j in ((sides, 0), (sides + tile_rows, cols - 1)):
        first = (j // 8) * piece + j % 8
        for block in range(GRID):
            mixed[at + block * span : at + (block + 1) * span] = came_ref[block, pl.ds(first, span, stride=8), :]
        mixed[at : at + tile_rows] += cot_ref[:, j, :]
    grad = dot3(mixed[...], weight_ref[...], NT)
    at = 0
    for depth_ref, grad_ref in (
        (top_ref, grad_top_ref), (bottom_ref, grad_bottom_ref), (left_ref, grad_left_ref), (right_ref, grad_right_ref)
    ):
        depth_out = depth_ref[...]
        grad_ref[...] = grad[at : at + depth_out.shape[0]] * gelu_slope(depth_out, gate(depth_out))
        at += depth_out.shape[0]


def edges(came, cot, depth_edges, weight):
    tile_rows, tile_cols, channels = cot.shape
    wide = weight.shape[0]
    vmem = pl.BlockSpec(memory_space=pltpu.VMEM)
    return call(
        edges_body,
        (),
        [vmem] * 7,
        [vmem] * 4,
        [shape(*a.shape) for a in depth_edges],
        scratch=[pltpu.VMEM((2 * tile_cols + 2 * tile_rows, channels), F32)],
        flops=12 * (tile_cols + tile_rows) * channels * wide,
        bytes_accessed=2**21,
        limit=56,
    )(came, cot, *depth_edges, weight)


def project_back_body(
    came_ref, cot_ref, depth_out_ref, weight_ref,
    grad_mixed_ref, grad_depth_ref, total_ref,
):
    step = pl.program_id(0)
    count, cols, wide = depth_out_ref.shape
    span = count // came_ref.shape[0]
    piece = span * 8

    @pl.when(step == 0)
    def _():
        total_ref[...] = jnp.zeros_like(total_ref)

    parts = []
    for i in range(count):
        block, inner = divmod(i, span)
        for k, cot in enumerate(load_row(cot_ref, (i,), cols)):
            parts.append(came_ref[block, pl.ds(inner * 8 + k, cols // 8, stride=piece), :] + cot)
    grad_mixed = jnp.concatenate(parts, axis=0)
    grad_mixed_ref[...] = grad_mixed.reshape(grad_mixed_ref.shape)
    mixed_split = split(grad_mixed)
    depth_out = depth_out_ref[...].reshape(count * cols, wide)
    gated = gate(depth_out)
    grad = dot3(mixed_split, weight_ref[...], NT) * gelu_slope(depth_out, gated)
    grad_depth_ref[...] = grad.reshape(count, cols, wide)
    total_ref[...] += dot3(mixed_split, depth_out * gated, TN)


def project_back(came, cot, depth_out, weight, count=8):
    tile_rows, tile_cols, wide = depth_out.shape
    channels = weight.shape[1]
    span = tile_rows // GRID
    tile = rows(count, tile_cols, channels)
    return call(
        project_back_body,
        (tile_rows // count,),
        [rows(count // span, span * tile_cols, channels), tile, rows(count, tile_cols, wide), whole(wide, channels)],
        [tile, rows(count, tile_cols, wide), whole(channels, wide)],
        [shape(tile_rows, tile_cols, channels), shape(tile_rows, tile_cols, wide), shape(channels, wide)],
        flops=12 * tile_rows * tile_cols * channels * wide,
        bytes_accessed=4 * tile_rows * tile_cols * (2 * wide + 3 * channels),
        limit=56,
    )(came, cot, depth_out, weight)


SLOTS = 16


def pack(refs, taps_ref, packed_ref):
    size = refs[0].shape[0]
    slot = 0
    for ref in refs:
        for lane in range(0, ref.shape[1], size):
            packed_ref[pl.ds(slot, size, stride=SLOTS), :] = ref[:, lane : lane + size]
            slot += 1
    taps = taps_ref.shape[0]
    empty = jnp.zeros((size, size), F32)
    packed_ref[pl.ds(slot, size, stride=SLOTS), :] = empty
    for k in range(taps_ref.shape[1] // size):
        packed_ref[pl.ds(slot + SLOTS * taps * k, taps, stride=SLOTS), :] = taps_ref[:, k * size : (k + 1) * size]
    for spare in range(slot + 1, SLOTS):
        packed_ref[pl.ds(spare, size, stride=SLOTS), :] = empty


def expand_back_body(
    inside_ref, grad_ref, before_ref, after_ref, top, bottom, left_ref, right_ref, pre_ref, field_ref, depth_ref,
    project_ref, qkv_ref, out_ref, bias_ref,
    grad_pre_ref, packed_ref, padded, left, right, grad_expand_ref, grad_depth_ref,
):
    step = pl.program_id(0)
    last = pl.num_programs(0) - 1
    count, cols, wide = grad_ref.shape

    @pl.when(step == 0)
    def _():
        grad_expand_ref[...] = jnp.zeros_like(grad_expand_ref)
        grad_depth_ref[...] = jnp.zeros_like(grad_depth_ref)
        left[...] = keep_column(left_ref[...], inside_ref[2], inside_ref[0], inside_ref[1])
        right[...] = keep_column(right_ref[...], inside_ref[3], inside_ref[0], inside_ref[1])

    def fill(at, row):
        edge = pl.ds(step * count + at, 1)
        fill_row(padded, at, row, left[edge, :], right[edge, :])

    fill(0, jnp.where(step == 0, keep_row(top[...], inside_ref[0]), before_ref[0]))
    fill(count + 1, jnp.where(step == last, keep_row(bottom[...], inside_ref[1]), after_ref[0]))
    for i in range(count):
        fill(i + 1, grad_ref[i])
    for lane in range(0, wide, 128):
        lanes = slice(lane, lane + 128)
        taps = [None] * 9
        for i in range(count):
            pre = pre_ref[i, :, lanes]
            gated = gate(pre)
            hidden = pre * gated
            total = None
            for tap in range(9):
                p, q = divmod(tap, 3)
                window = padded[i + 2 - p, 8 * (2 - q) : 8 * (2 - q) + cols, lanes]
                term = window * depth_ref[tap : tap + 1, lanes]
                total = term if total is None else total + term
                part = jnp.sum((window * hidden).reshape(cols // 8, 8, 128), axis=0)
                taps[tap] = part if taps[tap] is None else taps[tap] + part
            grad_pre_ref[i, :, lanes] = total * gelu_slope(pre, gated)
        for tap in range(9):
            grad_depth_ref[tap : tap + 1, lanes] += jnp.sum(taps[tap], axis=0, keepdims=True)
    normed, _ = normalize(load_rows(field_ref, cols))
    grad_expand_ref[...] += dot3(normed, grad_pre_ref[...].reshape(count * cols, wide), TN)

    @pl.when(step == last)
    def _():
        pack((grad_expand_ref, project_ref, qkv_ref, out_ref, bias_ref), grad_depth_ref, packed_ref)


def expand_back(flags, grad_depth_out, halo, pre, field, depth_weight, grads, count=8):
    tile_rows, tile_cols, channels = field.shape
    wide = pre.shape[2]
    edge = tile_rows + 2
    return call(
        expand_back_body,
        (tile_rows // count,),
        [
            pl.BlockSpec(memory_space=pltpu.SMEM),
            rows(count, tile_cols, wide),
            pl.BlockSpec((1, tile_cols, wide), lambda i: (jnp.maximum(count * i - 1, 0), 0, 0)),
            pl.BlockSpec((1, tile_cols, wide), lambda i: (jnp.minimum(count * i + count, tile_rows - 1), 0, 0)),
        ]
        + [whole(tile_cols, wide)] * 2
        + [whole(edge, wide)] * 2
        + [rows(count, tile_cols, wide), rows(count, tile_cols, channels), whole(9, wide)]
        + [whole(*a.shape) for a in grads],
        [rows(count, tile_cols, wide), whole(channels * SLOTS, channels)],
        [pltpu.HBM((tile_rows, tile_cols, wide), F32), shape(channels * SLOTS, channels)],
        scratch=[
            pltpu.VMEM((count + 2, tile_cols + 16, wide), F32),
            pltpu.VMEM((edge, wide), F32),
            pltpu.VMEM((edge, wide), F32),
            pltpu.VMEM((channels, wide), F32),
            pltpu.VMEM((16, wide), F32),
        ],
        flops=6 * tile_rows * tile_cols * channels * wide,
        bytes_accessed=4 * tile_rows * tile_cols * (3 * wide + channels),
        limit=56,
    )(flags, grad_depth_out, grad_depth_out, grad_depth_out, *halo, pre, field, depth_weight, *grads)


def finish_body(
    grad_pre_ref, field_ref, grad_mixed_ref, sent_ref, placed_ref, expand_ref, block_out_ref, grad_field_ref
):
    count, cols, wide = grad_pre_ref.shape
    span = count // sent_ref.shape[0]
    for i in range(count):
        block, inner = divmod(i, span)
        for c in range(cols // 8):
            there = slice(c * span * 8 + inner * 8, c * span * 8 + inner * 8 + 8)
            block_out_ref[i, 8 * c : 8 * c + 8, :] = sent_ref[block, there, :] + placed_ref[block, there, :]
    normed, scale = normalize(load_rows(field_ref, cols))
    grad_normed = dot3(grad_pre_ref[...].reshape(count * cols, wide), expand_ref[...], NT)
    grad_field = normalize_back(grad_normed, normed, scale) + grad_mixed_ref[...].reshape(count * cols, -1)
    for i in range(count):
        for k in range(8):
            here = i * cols + k * (cols // 8)
            grad_field_ref[i, pl.ds(k, cols // 8, stride=8), :] = grad_field[here : here + cols // 8]


def finish(grad_pre, field, grad_mixed, sent, placed, expand_weight, count=8):
    tile_rows, tile_cols, channels = field.shape
    wide = grad_pre.shape[2]
    span = tile_rows // GRID
    tile = rows(count, tile_cols, channels)
    blocks = rows(count // span, span * tile_cols, channels)
    return call(
        finish_body,
        (tile_rows // count,),
        [rows(count, tile_cols, wide), tile, tile, blocks, blocks, whole(channels, wide)],
        [tile, tile],
        [shape(*field.shape)] * 2,
        flops=6 * tile_rows * tile_cols * channels * wide,
        bytes_accessed=4 * tile_rows * tile_cols * (wide + 6 * channels),
        limit=56,
    )(grad_pre, field, grad_mixed, sent, placed, expand_weight)


def total_body(came_ref, total_ref):
    total = jnp.sum(came_ref[...], axis=0, keepdims=True)
    total_ref[...] = jnp.broadcast_to(total, total_ref.shape)


def unpack_body(packed_ref, expand_ref, project_ref, qkv_ref, out_ref, bias_ref, depth_ref):
    size = out_ref.shape[0]
    places = bias_ref.shape[1]

    def matrix(slot, count=size, first=0):
        return packed_ref[pl.ds(slot + SLOTS * first, count, stride=SLOTS), :]

    slot = 0
    for k in range(expand_ref.shape[1] // size):
        expand_ref[:, k * size : (k + 1) * size] = matrix(slot)
        slot += 1
    for k in range(project_ref.shape[0] // size):
        project_ref[k * size : (k + 1) * size, :] = matrix(slot).T
        slot += 1
    for k in range(qkv_ref.shape[1] // size):
        qkv_ref[:, k * size : (k + 1) * size] = matrix(slot)
        slot += 1
    out_ref[...] = matrix(slot)
    bias = matrix(slot + 1)
    for h in range(HEADS):
        at, lane = divmod(h, 2)
        bias_ref[h] = bias[at * places : (at + 1) * places, lane * places : (lane + 1) * places].T
    taps = 16
    for k in range(depth_ref.shape[1] // size):
        depth_ref[:, k * size : (k + 1) * size] = matrix(slot + 2, taps, taps * k)[: depth_ref.shape[0]]


def reduce_all(packed, like, after):
    size = packed.shape[1]
    vmem = pl.BlockSpec(memory_space=pltpu.VMEM)
    packed, after = lax.optimization_barrier((packed, after))
    came = lax.all_to_all(packed.reshape(size, SLOTS, size), ALL, 0, 0, tiled=True)
    total = call(total_body, (), [vmem], vmem, shape(size, SLOTS, size))(came)
    came = lax.all_to_all(total, ALL, 0, 0, tiled=True)
    totals = call(unpack_body, (), [vmem], [vmem] * 6, [shape(*a.shape) for a in like])(
        came.reshape(size * SLOTS, size)
    )
    return totals, after


def shift(values, axes, count, by):
    return lax.ppermute(values, axes, [(i, (i + by) % count) for i in range(count)])


def inside(row_count, col_count):
    row, col = lax.axis_index("row"), lax.axis_index(COLS)
    return jnp.stack([row > 0, row < row_count - 1, col > 0, col < col_count - 1]).astype(jnp.int32)


def beyond_rows(first, last, row_count):
    return shift(last, "row", row_count, 1), shift(first, "row", row_count, -1)


def beyond_columns(top, bottom, left, right, col_count):
    def column(edge, j):
        return jnp.concatenate([top[j : j + 1], edge, bottom[j : j + 1]], axis=0)

    end = top.shape[0] - 1
    return shift(column(right, end), COLS, col_count, 1), shift(column(left, 0), COLS, col_count, -1)


def swap(blocks):
    places = GRID * GRID
    flat = blocks.reshape(places, -1, blocks.shape[-1])
    return lax.all_to_all(flat, PAIRS, 0, 0, tiled=True)


def on_device(
    sizes, field, expand_weight, depth_weight, project_weight, qkv_weight, out_weight, pos_bias, cotangent
):
    places = GRID * GRID
    row_count, col_count = sizes
    flags = inside(row_count, col_count)
    halo = beyond_rows(field[0], field[-1], row_count)
    halo += beyond_columns(*halo, field[:, 0], field[:, -1], col_count)
    arranged, halo = lax.optimization_barrier((arrange(cotangent), halo))
    cot_grid = swap(arranged)
    sent, pre, depth_out, *depth_edges = forward(flags, field, halo, expand_weight, depth_weight, project_weight)
    mixed_grid = swap(sent)
    bias = pos_bias.transpose(2, 0, 1).reshape(places, HEADS * places)
    leave, mixture, grad_packed, grad_bias = attend(mixed_grid, cot_grid, qkv_weight, out_weight, bias)
    came = swap(leave)
    attended, grad_qkv, grad_out = attend_late(mixed_grid, cot_grid, mixture, grad_packed, out_weight)
    came, attended = lax.optimization_barrier((came, attended))
    came = came.reshape(sent.shape)
    first, last, left, right = edges(came, cotangent, depth_edges, project_weight)
    halo = beyond_rows(first, last, row_count)
    grad_mixed, grad_depth_out, grad_project = project_back(came, cotangent, depth_out, project_weight)
    halo, grad_depth_out = lax.optimization_barrier((halo, grad_depth_out))
    halo += beyond_columns(*halo, left, right, col_count)
    halo, attended = lax.optimization_barrier((halo, attended))
    placed = swap(attended).reshape(sent.shape)
    grad_pre, packed = expand_back(
        flags, grad_depth_out, halo, pre, field, depth_weight, (grad_project, grad_qkv, grad_out, grad_bias)
    )
    totals, placed = reduce_all(
        packed,
        (expand_weight, project_weight, qkv_weight, out_weight, pos_bias, depth_weight),
        placed,
    )
    grad_expand, grad_project, grad_qkv, grad_out, grad_bias, grad_depth = totals
    block_out, grad_field = finish(grad_pre, field, grad_mixed, sent, placed, expand_weight)
    return (
        block_out,
        grad_field,
        grad_expand,
        grad_depth,
        grad_project,
        grad_qkv,
        grad_out,
        grad_bias,
    )


def solution(mesh):
    row_count, col_count = mesh.devices.shape
    split_mesh = Mesh(mesh.devices.reshape(row_count, col_count // 2, 2), ALL)
    tile = P("row", COLS, None)
    return jax.shard_map(
        functools.partial(on_device, (row_count, col_count)),
        mesh=split_mesh,
        in_specs=(tile, P(), P(), P(), P(), P(), P(), tile),
        out_specs=(tile, tile, P(), P(), P(), P(), P(), P()),
        check_vma=False,
    )
```

```python
import functools

import jax
import jax.numpy as jnp
from jax import lax
from jax.experimental import pallas as pl
from jax.experimental.pallas import tpu as pltpu
from jax.sharding import Mesh, PartitionSpec as P

GRID = 8
HEADS = 4
ALL = ("row", "ch", "core")
COLS = ("ch", "core")
PAIRS = ("row", "ch")
K0 = 0.7978845608028654
K1 = K0 * 0.044715
F32 = jnp.float32
BF16 = jnp.bfloat16
NN = (((1,), (0,)), ((), ()))
NT = (((1,), (1,)), ((), ()))
TN = (((0,), (0,)), ((), ()))


def split(values):
    high = values.astype(BF16)
    return high, (values - high.astype(F32)).astype(BF16)


def dot(a, b, dims):
    return lax.dot_general(a, b, dims, preferred_element_type=F32)


def dot3(a, b, dims):
    a_high, a_low = a if isinstance(a, tuple) else split(a)
    b_high, b_low = b if isinstance(b, tuple) else split(b)
    (a_axis,), (b_axis,) = dims[0]
    return dot(
        jnp.concatenate([a_high, a_low, a_high], axis=a_axis),
        jnp.concatenate([b_high, b_high, b_low], axis=b_axis),
        dims,
    )


def normalize(values):
    center = values - jnp.mean(values, axis=-1, keepdims=True)
    spread = jnp.mean(center * center, axis=-1, keepdims=True)
    scale = lax.rsqrt(spread + 1e-05)
    return center * scale, scale


def normalize_back(grad, normed, scale):
    grad_mean = jnp.mean(grad, axis=-1, keepdims=True)
    along = jnp.mean(grad * normed, axis=-1, keepdims=True)
    return scale * (grad - grad_mean - normed * along)


def gate(values):
    return 0.5 + 0.5 * jnp.tanh(values * (K0 + K1 * (values * values)))


def gelu(values):
    return values * gate(values)


def gelu_slope(values, gated):
    return gated + 2.0 * values * (gated - gated * gated) * (K0 + (3.0 * K1) * (values * values))


def call(body, grid, in_specs, out_specs, out_shape, scratch=(), flops=0, bytes_accessed=0, limit=22):
    return pl.pallas_call(
        body,
        grid=grid,
        in_specs=in_specs,
        out_specs=out_specs,
        out_shape=out_shape,
        scratch_shapes=list(scratch),
        compiler_params=pltpu.CompilerParams(vmem_limit_bytes=limit * 2**20),
        cost_estimate=pl.CostEstimate(
            flops=flops, bytes_accessed=bytes_accessed, transcendentals=0
        ),
    )


def shape(*dims):
    return jax.ShapeDtypeStruct(dims, F32)


def whole(*dims):
    return pl.BlockSpec(dims, lambda *_: (0,) * len(dims))


def rows(*dims):
    return pl.BlockSpec(dims, lambda i: (i,) + (0,) * (len(dims) - 1))


def load_row(ref, lead, cols):
    return [ref[lead + (pl.ds(k, cols // 8, stride=8),)] for k in range(8)]


def load_rows(ref, cols):
    return jnp.concatenate(
        [part for i in range(ref.shape[0]) for part in load_row(ref, (i,), cols)], axis=0
    )


def fill_row(padded, at, row, left, right):
    cols = row.shape[0]
    padded[at, 8 : 8 + cols, :] = row
    padded[at, 0:1, :] = left
    padded[at, 1:8, :] = row[cols - 8 : cols - 1]
    padded[at, 8 + cols : 15 + cols, :] = row[1:8]
    padded[at, 15 + cols : 16 + cols, :] = right


def keep_row(values, flag):
    return jnp.where(flag > 0, values, 0.0)


def keep_column(values, flag, above, below):
    at = lax.broadcasted_iota(jnp.int32, values.shape, 0)
    kept = jnp.where(at == 0, above, jnp.where(at == values.shape[0] - 1, below, 1)) * flag
    return jnp.where(kept > 0, values, 0.0)


def forward_body(
    inside_ref, field_ref, late_ref, top_ref, bottom_ref, left_ref, right_ref, expand_ref, depth_ref, weight_ref,
    sent_ref, pre_ref, depth_out_ref, depth_top_ref, depth_bottom_ref, depth_left_ref, depth_right_ref,
    padded, left, right,
):
    step = pl.program_id(0)
    last = pl.num_programs(0) - 1
    count, cols, channels = field_ref.shape
    wide = expand_ref.shape[1]
    total_rows = padded.shape[0] - 2

    @pl.when(step == 0)
    def _():
        weight = split(expand_ref[...])

        def hidden(values):
            return gelu(dot3(normalize(values)[0], weight, NN))

        above, below = inside_ref[0], inside_ref[1]
        left[...] = hidden(keep_column(left_ref[...], inside_ref[2], above, below))
        right[...] = hidden(keep_column(right_ref[...], inside_ref[3], above, below))
        for at, ref, flag in ((0, top_ref, above), (total_rows + 1, bottom_ref, below)):
            row = hidden(keep_row(jnp.concatenate(load_row(ref, (), cols), axis=0), flag))
            fill_row(padded, at, row, left[at : at + 1, :], right[at : at + 1, :])

    @pl.when(step < last)
    def _():
        normed, _ = normalize(load_rows(field_ref, cols))
        pre = dot3(normed, expand_ref[...], NN)
        pre_ref[...] = pre.reshape(count, cols, wide)
        hidden = gelu(pre)
        for i in range(count):
            at = step * count + i + 1
            row = hidden[i * cols : (i + 1) * cols]
            fill_row(padded, at, row, left[pl.ds(at, 1), :], right[pl.ds(at, 1), :])

    @pl.when(step > 0)
    def _():
        start = (step - 1) * count
        for lane in range(0, wide, 128):
            lanes = slice(lane, lane + 128)
            for i in range(count):
                total = None
                for p in range(3):
                    for q in range(3):
                        term = padded[start + i + p, 8 * q : 8 * q + cols, lanes] * depth_ref[3 * p + q : 3 * p + q + 1, lanes]
                        total = term if total is None else total + term
                depth_out_ref[i, :, lanes] = total
        depth_left_ref[...] = depth_out_ref[:, 0, :]
        depth_right_ref[...] = depth_out_ref[:, cols - 1, :]
        activated = gelu(depth_out_ref[...].reshape(count * cols, wide))
        mixed = dot3(activated, weight_ref[...], NN) + load_rows(late_ref, cols)
        span = total_rows // GRID
        for i in range(count):
            block, inner = divmod(i, span)
            for k in range(8):
                here = i * cols + k * (cols // 8)
                sent_ref[block, pl.ds(inner * 8 + k, cols // 8, stride=span * 8), :] = mixed[
                    here : here + cols // 8
                ]

    @pl.when(step == 1)
    def _():
        depth_top_ref[...] = depth_out_ref[0]

    @pl.when(step == last)
    def _():
        depth_bottom_ref[...] = depth_out_ref[count - 1]


def forward(flags, field, halo, expand_weight, depth_weight, weight, count=8):
    tile_rows, tile_cols, channels = field.shape
    wide = expand_weight.shape[1]
    span = tile_rows // GRID
    steps = tile_rows // count
    edge = tile_rows + 2

    def early(*dims):
        return pl.BlockSpec(dims, lambda i: (jnp.minimum(i, steps - 1),) + (0,) * (len(dims) - 1))

    def late(*dims):
        return pl.BlockSpec(dims, lambda i: (jnp.maximum(i - 1, 0),) + (0,) * (len(dims) - 1))

    return call(
        forward_body,
        (steps + 1,),
        [pl.BlockSpec(memory_space=pltpu.SMEM), early(count, tile_cols, channels), late(count, tile_cols, channels)]
        + [whole(tile_cols, channels)] * 2
        + [whole(edge, channels)] * 2
        + [whole(channels, wide), whole(9, wide), whole(wide, channels)],
        [
            late(count // span, span * tile_cols, channels),
            early(count, tile_cols, wide),
            late(count, tile_cols, wide),
            whole(tile_cols, wide),
            whole(tile_cols, wide),
            late(count, wide),
            late(count, wide),
        ],
        [
            shape(GRID, span * tile_cols, channels),
            pltpu.HBM((tile_rows, tile_cols, wide), F32),
            pltpu.HBM((tile_rows, tile_cols, wide), F32),
            pltpu.HBM((tile_cols, wide), F32),
            pltpu.HBM((tile_cols, wide), F32),
            pltpu.HBM((tile_rows, wide), F32),
            pltpu.HBM((tile_rows, wide), F32),
        ],
        scratch=[
            pltpu.VMEM((edge, tile_cols + 16, wide), F32),
            pltpu.VMEM((edge, wide), F32),
            pltpu.VMEM((edge, wide), F32),
        ],
        flops=12 * tile_rows * tile_cols * channels * wide,
        bytes_accessed=4 * tile_rows * tile_cols * (2 * wide + 3 * channels),
    )(flags, field, field, *halo, expand_weight, depth_weight, weight)


def arrange_body(tile_ref, sent_ref):
    tile_rows, cols, _ = tile_ref.shape
    span = tile_rows // GRID
    for i in range(tile_rows):
        block, inner = divmod(i, span)
        for c in range(cols // 8):
            there = c * span * 8 + inner * 8
            sent_ref[block, there : there + 8, :] = tile_ref[i, 8 * c : 8 * c + 8, :]


def arrange(tile):
    tile_rows, tile_cols, channels = tile.shape
    vmem = pl.BlockSpec(memory_space=pltpu.VMEM)
    return call(arrange_body, (), [vmem], vmem, shape(GRID, tile_rows * tile_cols // GRID, channels))(tile)


SPARE = 8


def pitched(ref, lead, first, count, pitch, groups):
    return jnp.concatenate(
        [ref[lead + (pl.ds(pl.multiple_of((first + j) * pitch, 8), groups),)] for j in range(count)], axis=0
    )


def attend_body(
    mixed_ref, cot_ref, qkv_ref, out_ref, bias_ref,
    leave_ref, mixture_out, grad_packed_out, grad_bias_out,
    packed_ref, delta_ref, mixture_ref, grad_packed_ref, bias_total, grad_bias_ref, done,
):
    places, groups, channels = mixed_ref.shape
    head = channels // HEADS
    scale = head ** (-0.5)
    pitch = groups + SPARE
    step = 32
    rows_in = step * groups
    together = 4

    def chunk(i, ref):
        return ref[pl.ds(i * step, step)].reshape(rows_in, channels)

    def prepare(i, carry):
        normed, _ = normalize(chunk(i, mixed_ref))
        packed = dot3(normed, qkv_ref[...], NN)
        delta = dot3(chunk(i, cot_ref), out_ref[...], NT)
        for j in range(step):
            here = pl.ds(pl.multiple_of((i * step + j) * pitch, 8), groups)
            part = slice(j * groups, (j + 1) * groups)
            packed_ref[0, here, :] = packed[part, :channels] * scale
            packed_ref[1, here, :] = packed[part, channels : 2 * channels]
            packed_ref[2, here, :] = packed[part, 2 * channels :]
            delta_ref[here, :] = delta[part]
        return carry

    lax.fori_loop(0, places // step, prepare, 0)
    bias_total[...] = jnp.zeros_like(bias_total)

    head_of = lax.broadcasted_iota(jnp.int32, (places, channels), 1) // head

    def spread(values):
        return jnp.concatenate(
            [jnp.where(head_of == h, values, 0.0).astype(BF16) for h in range(HEADS)], axis=0
        )

    def spread_split(values):
        high, low = split(values)
        return spread(high.astype(F32)), spread(low.astype(F32))

    def gather_heads(wide):
        total = jnp.where(head_of == 0, wide[:places], 0.0)
        for h in range(1, HEADS):
            total = total + jnp.where(head_of == h, wide[h * places : (h + 1) * places], 0.0)
        return total

    def some_groups(i, carry):
        here = [pl.ds(i * together + k, places, stride=pitch) for k in range(together)]
        query = [spread_split(packed_ref[0, h, :]) for h in here]
        delta = [spread_split(delta_ref[h, :]) for h in here]
        key = [split(packed_ref[1, h, :]) for h in here]
        value = [split(packed_ref[2, h, :]) for h in here]
        scores = [dot3(a, b, NT) + bias_ref[...] for a, b in zip(key, query)]
        grad_weights = [dot3(a, b, NT) for a, b in zip(value, delta)]
        powers = [jnp.exp(s - jnp.max(s, axis=0, keepdims=True)) for s in scores]
        weights = [p * (1.0 / jnp.sum(p, axis=0, keepdims=True)) for p in powers]
        along = [jnp.sum(w * g, axis=0, keepdims=True) for w, g in zip(weights, grad_weights)]
        grad_scores = [w * (g - a) for w, g, a in zip(weights, grad_weights, along)]
        weights = [split(w) for w in weights]
        grad_split = [split(g) for g in grad_scores]
        mixture = [gather_heads(dot3(w, v, TN)) for w, v in zip(weights, value)]
        grad_value = [dot3(w, d, NN) for w, d in zip(weights, delta)]
        grad_key = [dot3(g, q, NN) for g, q in zip(grad_split, query)]
        grad_query = [gather_heads(dot3(g, k, TN)) * scale for g, k in zip(grad_split, key)]
        for k, h in enumerate(here):
            mixture_ref[h, :] = mixture[k]
            grad_packed_ref[0, h, :] = grad_query[k]
            grad_packed_ref[1, h, :] = grad_key[k]
            grad_packed_ref[2, h, :] = grad_value[k]
        bias_total[...] += functools.reduce(jnp.add, grad_scores)
        return carry

    lax.fori_loop(0, groups // together, some_groups, 0)

    half = bias_total.shape[1] // 2
    grad_bias_ref[:places, :] = bias_total[:, :half]
    grad_bias_ref[places:, :] = bias_total[:, half:]
    copies = [
        pltpu.make_async_copy(mixture_ref, mixture_out, done.at[0]),
        pltpu.make_async_copy(grad_packed_ref, grad_packed_out, done.at[1]),
        pltpu.make_async_copy(grad_bias_ref, grad_bias_out, done.at[2]),
    ]
    for copy in copies:
        copy.start()

    def finish(i, carry):
        normed, spread_scale = normalize(chunk(i, mixed_ref))
        grad = jnp.concatenate(
            [pitched(grad_packed_ref, (k,), i * step, step, pitch, groups) for k in range(3)], axis=1
        )
        grad_in = normalize_back(dot3(grad, qkv_ref[...], NT), normed, spread_scale)
        leave_ref[pl.ds(i * step, step)] = grad_in.reshape(step, groups, channels)
        return carry

    lax.fori_loop(0, places // step, finish, 0)
    for copy in copies:
        copy.wait()


def attend(mixed, cot, qkv_weight, out_weight, bias):
    places, groups, channels = mixed.shape
    tokens = places * groups
    padded = places * (groups + SPARE)
    vmem = pl.BlockSpec(memory_space=pltpu.VMEM)
    return call(
        attend_body,
        (),
        [vmem] * 5,
        [vmem] + [pl.BlockSpec(memory_space=pl.ANY)] * 3,
        [
            shape(places, groups, channels), pltpu.HBM((padded, channels), F32), pltpu.HBM((3, padded, channels), F32),
            pltpu.HBM((2 * places, bias.shape[1] // 2), F32),
        ],
        scratch=[
            pltpu.VMEM((3, padded, channels), F32),
            pltpu.VMEM((padded, channels), F32),
            pltpu.VMEM((padded, channels), F32),
            pltpu.VMEM((3, padded, channels), F32),
            pltpu.VMEM(bias.shape, F32),
            pltpu.VMEM((2 * places, bias.shape[1] // 2), F32),
            pltpu.SemaphoreType.DMA((3,)),
        ],
        flops=6 * tokens * channels * (12 * channels + 6 * places),
        bytes_accessed=16 * tokens * channels,
    )(mixed, cot, qkv_weight, out_weight, bias)


def attend_late_body(
    mixed_ref, cot_ref, mixture_ref, grad_packed_ref, out_ref, attended_ref, grad_qkv_ref, grad_out_ref
):
    @pl.when(pl.program_id(0) == 0)
    def _():
        grad_qkv_ref[...] = jnp.zeros_like(grad_qkv_ref)
        grad_out_ref[...] = jnp.zeros_like(grad_out_ref)

    step, groups, channels = mixed_ref.shape
    pitch = groups + SPARE
    mixture = split(pitched(mixture_ref, (), 0, step, pitch, groups))
    attended_ref[...] = dot3(mixture, out_ref[...], NN).reshape(attended_ref.shape)
    grad_out_ref[...] += dot3(mixture, cot_ref[...].reshape(step * groups, channels), TN)
    normed, _ = normalize(mixed_ref[...].reshape(step * groups, channels))
    grad = jnp.concatenate(
        [pitched(grad_packed_ref, (k,), 0, step, pitch, groups) for k in range(3)], axis=1
    )
    grad_qkv_ref[...] += dot3(normed, grad, TN)


def attend_late(mixed, cot, mixture, grad_packed, out_weight, step=16):
    places, groups, channels = mixed.shape
    tile = rows(step, groups, channels)
    return call(
        attend_late_body,
        (places // step,),
        [
            tile, tile, rows(step * (groups + SPARE), channels),
            pl.BlockSpec((3, step * (groups + SPARE), channels), lambda i: (0, i, 0)), whole(channels, channels),
        ],
        [tile, whole(channels, 3 * channels), whole(channels, channels)],
        [shape(places, groups, channels), shape(channels, 3 * channels), shape(channels, channels)],
        flops=30 * places * groups * channels * channels,
        bytes_accessed=28 * places * groups * channels,
    )(mixed, cot, mixture, grad_packed, out_weight)


def edges_body(
    came_ref, cot_ref, top_ref, bottom_ref, left_ref, right_ref, weight_ref,
    grad_top_ref, grad_bottom_ref, grad_left_ref, grad_right_ref, mixed,
):
    tile_rows, cols, _ = cot_ref.shape
    span = tile_rows // GRID
    piece = span * 8
    sides = 2 * cols
    for at, i in ((0, 0), (cols, tile_rows - 1)):
        block, inner = divmod(i, span)
        for k in range(8):
            here = at + k * (cols // 8)
            mixed[here : here + cols // 8] = (
                came_ref[block, pl.ds(inner * 8 + k, cols // 8, stride=piece), :]
                + cot_ref[i, pl.ds(k, cols // 8, stride=8), :]
            )
    for at, j in ((sides, 0), (sides + tile_rows, cols - 1)):
        first = (j // 8) * piece + j % 8
        for block in range(GRID):
            mixed[at + block * span : at + (block + 1) * span] = came_ref[block, pl.ds(first, span, stride=8), :]
        mixed[at : at + tile_rows] += cot_ref[:, j, :]
    grad = dot3(mixed[...], weight_ref[...], NT)
    at = 0
    for depth_ref, grad_ref in (
        (top_ref, grad_top_ref), (bottom_ref, grad_bottom_ref), (left_ref, grad_left_ref), (right_ref, grad_right_ref)
    ):
        depth_out = depth_ref[...]
        grad_ref[...] = grad[at : at + depth_out.shape[0]] * gelu_slope(depth_out, gate(depth_out))
        at += depth_out.shape[0]


def edges(came, cot, depth_edges, weight):
    tile_rows, tile_cols, channels = cot.shape
    wide = weight.shape[0]
    vmem = pl.BlockSpec(memory_space=pltpu.VMEM)
    return call(
        edges_body,
        (),
        [vmem] * 7,
        [vmem] * 4,
        [shape(*a.shape) for a in depth_edges],
        scratch=[pltpu.VMEM((2 * tile_cols + 2 * tile_rows, channels), F32)],
        flops=12 * (tile_cols + tile_rows) * channels * wide,
        bytes_accessed=2**21,
        limit=56,
    )(came, cot, *depth_edges, weight)


def project_back_body(
    came_ref, cot_ref, depth_out_ref, weight_ref,
    grad_mixed_ref, grad_depth_ref, total_ref,
):
    step = pl.program_id(0)
    count, cols, wide = depth_out_ref.shape
    span = count // came_ref.shape[0]
    piece = span * 8

    @pl.when(step == 0)
    def _():
        total_ref[...] = jnp.zeros_like(total_ref)

    parts = []
    for i in range(count):
        block, inner = divmod(i, span)
        for k, cot in enumerate(load_row(cot_ref, (i,), cols)):
            parts.append(came_ref[block, pl.ds(inner * 8 + k, cols // 8, stride=piece), :] + cot)
    grad_mixed = jnp.concatenate(parts, axis=0)
    grad_mixed_ref[...] = grad_mixed.reshape(grad_mixed_ref.shape)
    mixed_split = split(grad_mixed)
    depth_out = depth_out_ref[...].reshape(count * cols, wide)
    gated = gate(depth_out)
    grad = dot3(mixed_split, weight_ref[...], NT) * gelu_slope(depth_out, gated)
    grad_depth_ref[...] = grad.reshape(count, cols, wide)
    total_ref[...] += dot3(mixed_split, depth_out * gated, TN)


def project_back(came, cot, depth_out, weight, count=8):
    tile_rows, tile_cols, wide = depth_out.shape
    channels = weight.shape[1]
    span = tile_rows // GRID
    tile = rows(count, tile_cols, channels)
    return call(
        project_back_body,
        (tile_rows // count,),
        [rows(count // span, span * tile_cols, channels), tile, rows(count, tile_cols, wide), whole(wide, channels)],
        [tile, rows(count, tile_cols, wide), whole(channels, wide)],
        [shape(tile_rows, tile_cols, channels), shape(tile_rows, tile_cols, wide), shape(channels, wide)],
        flops=12 * tile_rows * tile_cols * channels * wide,
        bytes_accessed=4 * tile_rows * tile_cols * (2 * wide + 3 * channels),
        limit=56,
    )(came, cot, depth_out, weight)


SLOTS = 16


def pack(refs, taps_ref, target, half):
    size = refs[0].shape[0] // 2
    own = pl.ds(pl.multiple_of(half * size, size), size)
    slot = 0
    for ref in refs:
        for lane in range(0, ref.shape[1], 2 * size):
            target[pl.ds(slot, size, stride=SLOTS), :] = ref[own, lane : lane + 2 * size]
            slot += 1
    target[pl.ds(slot, size, stride=SLOTS), :] = taps_ref[own, :]
    for spare in range(slot + 1, SLOTS):
        target[pl.ds(spare, size, stride=SLOTS), :] = jnp.zeros((size, 2 * size), F32)


def expand_back_body(
    inside_ref, grad_ref, before_ref, after_ref, top, bottom, left_ref, right_ref, pre_ref, field_ref, depth_ref,
    project_ref, qkv_ref, out_ref, bias_ref,
    grad_pre_ref, kept_ref, given_ref, padded, left, right, grad_expand_ref, grad_depth_ref, taps_ref,
):
    step = pl.program_id(0)
    last = pl.num_programs(0) - 1
    count, cols, wide = grad_ref.shape

    @pl.when(step == 0)
    def _():
        grad_expand_ref[...] = jnp.zeros_like(grad_expand_ref)
        grad_depth_ref[...] = jnp.zeros_like(grad_depth_ref)
        left[...] = keep_column(left_ref[...], inside_ref[2], inside_ref[0], inside_ref[1])
        right[...] = keep_column(right_ref[...], inside_ref[3], inside_ref[0], inside_ref[1])

    def fill(at, row):
        edge = pl.ds(step * count + at, 1)
        fill_row(padded, at, row, left[edge, :], right[edge, :])

    fill(0, jnp.where(step == 0, keep_row(top[...], inside_ref[0]), before_ref[0]))
    fill(count + 1, jnp.where(step == last, keep_row(bottom[...], inside_ref[1]), after_ref[0]))
    for i in range(count):
        fill(i + 1, grad_ref[i])
    for lane in range(0, wide, 128):
        lanes = slice(lane, lane + 128)
        taps = [None] * 9
        for i in range(count):
            pre = pre_ref[i, :, lanes]
            gated = gate(pre)
            hidden = pre * gated
            total = None
            for tap in range(9):
                p, q = divmod(tap, 3)
                window = padded[i + 2 - p, 8 * (2 - q) : 8 * (2 - q) + cols, lanes]
                term = window * depth_ref[tap : tap + 1, lanes]
                total = term if total is None else total + term
                part = jnp.sum((window * hidden).reshape(cols // 8, 8, 128), axis=0)
                taps[tap] = part if taps[tap] is None else taps[tap] + part
            grad_pre_ref[i, :, lanes] = total * gelu_slope(pre, gated)
        for tap in range(9):
            grad_depth_ref[tap : tap + 1, lanes] += jnp.sum(taps[tap], axis=0, keepdims=True)
    normed, _ = normalize(load_rows(field_ref, cols))
    grad_expand_ref[...] += dot3(normed, grad_pre_ref[...].reshape(count * cols, wide), TN)

    @pl.when(step == last)
    def _():
        taps_ref[...] = jnp.zeros_like(taps_ref)
        taps, size = grad_depth_ref.shape[0], taps_ref.shape[1]
        for k in range(wide // size):
            taps_ref[k * taps : (k + 1) * taps, :] = grad_depth_ref[:, k * size : (k + 1) * size]
        refs = (grad_expand_ref, project_ref, qkv_ref, out_ref, bias_ref)
        pack(refs, taps_ref, kept_ref, inside_ref[4])
        pack(refs, taps_ref, given_ref, 1 - inside_ref[4])


def expand_back(flags, grad_depth_out, halo, pre, field, depth_weight, grads, count=8):
    tile_rows, tile_cols, channels = field.shape
    wide = pre.shape[2]
    edge = tile_rows + 2
    return call(
        expand_back_body,
        (tile_rows // count,),
        [
            pl.BlockSpec(memory_space=pltpu.SMEM),
            rows(count, tile_cols, wide),
            pl.BlockSpec((1, tile_cols, wide), lambda i: (jnp.maximum(count * i - 1, 0), 0, 0)),
            pl.BlockSpec((1, tile_cols, wide), lambda i: (jnp.minimum(count * i + count, tile_rows - 1), 0, 0)),
        ]
        + [whole(tile_cols, wide)] * 2
        + [whole(edge, wide)] * 2
        + [rows(count, tile_cols, wide), rows(count, tile_cols, channels), whole(9, wide)]
        + [whole(*a.shape) for a in grads],
        [rows(count, tile_cols, wide)] + [whole(channels // 2 * SLOTS, channels)] * 2,
        [pltpu.HBM((tile_rows, tile_cols, wide), F32)] + [shape(channels // 2 * SLOTS, channels)] * 2,
        scratch=[
            pltpu.VMEM((count + 2, tile_cols + 16, wide), F32),
            pltpu.VMEM((edge, wide), F32),
            pltpu.VMEM((edge, wide), F32),
            pltpu.VMEM((channels, wide), F32),
            pltpu.VMEM((16, wide), F32),
            pltpu.VMEM((channels, channels), F32),
        ],
        flops=6 * tile_rows * tile_cols * channels * wide,
        bytes_accessed=4 * tile_rows * tile_cols * (3 * wide + channels),
        limit=56,
    )(flags, grad_depth_out, grad_depth_out, grad_depth_out, *halo, pre, field, depth_weight, *grads)


def finish_body(
    grad_pre_ref, field_ref, grad_mixed_ref, sent_ref, placed_ref, expand_ref, block_out_ref, grad_field_ref
):
    count, cols, wide = grad_pre_ref.shape
    span = count // sent_ref.shape[0]
    for i in range(count):
        block, inner = divmod(i, span)
        for c in range(cols // 8):
            there = slice(c * span * 8 + inner * 8, c * span * 8 + inner * 8 + 8)
            block_out_ref[i, 8 * c : 8 * c + 8, :] = sent_ref[block, there, :] + placed_ref[block, there, :]
    normed, scale = normalize(load_rows(field_ref, cols))
    grad_normed = dot3(grad_pre_ref[...].reshape(count * cols, wide), expand_ref[...], NT)
    grad_field = normalize_back(grad_normed, normed, scale) + grad_mixed_ref[...].reshape(count * cols, -1)
    for i in range(count):
        for k in range(8):
            here = i * cols + k * (cols // 8)
            grad_field_ref[i, pl.ds(k, cols // 8, stride=8), :] = grad_field[here : here + cols // 8]


def finish(grad_pre, field, grad_mixed, sent, placed, expand_weight, count=8):
    tile_rows, tile_cols, channels = field.shape
    wide = grad_pre.shape[2]
    span = tile_rows // GRID
    tile = rows(count, tile_cols, channels)
    blocks = rows(count // span, span * tile_cols, channels)
    return call(
        finish_body,
        (tile_rows // count,),
        [rows(count, tile_cols, wide), tile, tile, blocks, blocks, whole(channels, wide)],
        [tile, tile],
        [shape(*field.shape)] * 2,
        flops=6 * tile_rows * tile_cols * channels * wide,
        bytes_accessed=4 * tile_rows * tile_cols * (wide + 6 * channels),
        limit=56,
    )(grad_pre, field, grad_mixed, sent, placed, expand_weight)


def total_body(came_ref, total_ref):
    total = jnp.sum(came_ref[...], axis=0, keepdims=True)
    total_ref[...] = jnp.broadcast_to(total, total_ref.shape)


def unpack_body(inside_ref, mine_ref, other_ref, expand_ref, project_ref, qkv_ref, out_ref, bias_ref, depth_ref):
    size = out_ref.shape[0]
    places = bias_ref.shape[1]

    def matrix(slot):
        here = pl.ds(slot, size // 2, stride=SLOTS)
        mine, other = mine_ref[here, :], other_ref[here, :]
        second = inside_ref[4] > 0
        return jnp.concatenate([jnp.where(second, other, mine), jnp.where(second, mine, other)], axis=0)

    slot = 0
    for k in range(expand_ref.shape[1] // size):
        expand_ref[:, k * size : (k + 1) * size] = matrix(slot)
        slot += 1
    for k in range(project_ref.shape[0] // size):
        project_ref[k * size : (k + 1) * size, :] = matrix(slot).T
        slot += 1
    for k in range(qkv_ref.shape[1] // size):
        qkv_ref[:, k * size : (k + 1) * size] = matrix(slot)
        slot += 1
    out_ref[...] = matrix(slot)
    bias = matrix(slot + 1)
    for h in range(HEADS):
        at, lane = divmod(h, 2)
        bias_ref[h] = bias[at * places : (at + 1) * places, lane * places : (lane + 1) * places].T
    taps = matrix(slot + 2)
    for k in range(depth_ref.shape[1] // size):
        depth_ref[:, k * size : (k + 1) * size] = taps[16 * k : 16 * k + depth_ref.shape[0]]


def reduce_all(flags, kept, given, like, after, beside):
    size = kept.shape[1]
    chips = size // 2
    vmem = pl.BlockSpec(memory_space=pltpu.VMEM)
    pair = [(0, 1), (1, 0)]
    own = kept + lax.ppermute(given, "core", pair)
    own, after = lax.optimization_barrier((own, after))
    came = lax.all_to_all(own.reshape(chips, SLOTS, size), PAIRS, 0, 0, tiled=True)
    total = call(total_body, (), [vmem], vmem, shape(chips, SLOTS, size))(came)
    mine = lax.all_to_all(total, PAIRS, 0, 0, tiled=True).reshape(chips * SLOTS, size)
    mine, others = lax.optimization_barrier((mine, beside(after)))
    other = lax.ppermute(mine, "core", pair)
    totals = call(
        unpack_body,
        (),
        [pl.BlockSpec(memory_space=pltpu.SMEM), vmem, vmem],
        [vmem] * 6,
        [shape(*a.shape) for a in like],
    )(flags, mine, other)
    return totals, others


def shift(values, axes, count, by):
    return lax.ppermute(values, axes, [(i, (i + by) % count) for i in range(count)])


def inside(row_count, col_count):
    row, col = lax.axis_index("row"), lax.axis_index(COLS)
    second = lax.axis_index("core") > 0
    return jnp.stack([row > 0, row < row_count - 1, col > 0, col < col_count - 1, second]).astype(jnp.int32)


def beyond_rows(first, last, row_count):
    return shift(last, "row", row_count, 1), shift(first, "row", row_count, -1)


def beyond_columns(top, bottom, left, right, col_count):
    def column(edge, j):
        return jnp.concatenate([top[j : j + 1], edge, bottom[j : j + 1]], axis=0)

    end = top.shape[0] - 1
    return shift(column(right, end), COLS, col_count, 1), shift(column(left, 0), COLS, col_count, -1)


def swap(blocks):
    places = GRID * GRID
    flat = blocks.reshape(places, -1, blocks.shape[-1])
    return lax.all_to_all(flat, PAIRS, 0, 0, tiled=True)


def on_device(
    sizes, field, expand_weight, depth_weight, project_weight, qkv_weight, out_weight, pos_bias, cotangent
):
    places = GRID * GRID
    row_count, col_count = sizes
    flags = inside(row_count, col_count)
    halo = beyond_rows(field[0], field[-1], row_count)
    halo += beyond_columns(*halo, field[:, 0], field[:, -1], col_count)
    arranged, halo = lax.optimization_barrier((arrange(cotangent), halo))
    cot_grid = swap(arranged)
    sent, pre, depth_out, *depth_edges = forward(flags, field, halo, expand_weight, depth_weight, project_weight)
    mixed_grid = swap(sent)
    bias = pos_bias.transpose(2, 0, 1).reshape(places, HEADS * places)
    leave, mixture, grad_packed, grad_bias = attend(mixed_grid, cot_grid, qkv_weight, out_weight, bias)
    came = swap(leave)
    attended, grad_qkv, grad_out = attend_late(mixed_grid, cot_grid, mixture, grad_packed, out_weight)
    came, attended = lax.optimization_barrier((came, attended))
    came = came.reshape(sent.shape)
    first, last, left, right = edges(came, cotangent, depth_edges, project_weight)
    halo = beyond_rows(first, last, row_count)
    grad_mixed, grad_depth_out, grad_project = project_back(came, cotangent, depth_out, project_weight)
    halo, grad_depth_out = lax.optimization_barrier((halo, grad_depth_out))
    halo += beyond_columns(*halo, left, right, col_count)
    halo, attended = lax.optimization_barrier((halo, attended))
    placed = swap(attended).reshape(sent.shape)
    grad_pre, kept, given = expand_back(
        flags, grad_depth_out, halo, pre, field, depth_weight, (grad_project, grad_qkv, grad_out, grad_bias)
    )
    totals, (block_out, grad_field) = reduce_all(
        flags,
        kept,
        given,
        (expand_weight, project_weight, qkv_weight, out_weight, pos_bias, depth_weight),
        placed,
        lambda placed: finish(grad_pre, field, grad_mixed, sent, placed, expand_weight),
    )
    grad_expand, grad_project, grad_qkv, grad_out, grad_bias, grad_depth = totals
    return (
        block_out,
        grad_field,
        grad_expand,
        grad_depth,
        grad_project,
        grad_qkv,
        grad_out,
        grad_bias,
    )


def solution(mesh):
    row_count, col_count = mesh.devices.shape
    split_mesh = Mesh(mesh.devices.reshape(row_count, col_count // 2, 2), ALL)
    tile = P("row", COLS, None)
    return jax.shard_map(
        functools.partial(on_device, (row_count, col_count)),
        mesh=split_mesh,
        in_specs=(tile, P(), P(), P(), P(), P(), P(), tile),
        out_specs=(tile, tile, P(), P(), P(), P(), P(), P()),
        check_vma=False,
    )
```

```python
import functools

import jax
import jax.numpy as jnp
from jax import lax
from jax.experimental import pallas as pl
from jax.experimental.pallas import tpu as pltpu
from jax.sharding import Mesh, PartitionSpec as P

GRID = 8
HEADS = 4
ALL = ("row", "ch", "core")
COLS = ("ch", "core")
PAIRS = ("row", "ch")
K0 = 0.7978845608028654
K1 = K0 * 0.044715
F32 = jnp.float32
BF16 = jnp.bfloat16
NN = (((1,), (0,)), ((), ()))
NT = (((1,), (1,)), ((), ()))
TN = (((0,), (0,)), ((), ()))


def split(values):
    high = values.astype(BF16)
    return high, (values - high.astype(F32)).astype(BF16)


def dot(a, b, dims):
    return lax.dot_general(a, b, dims, preferred_element_type=F32)


def dot3(a, b, dims):
    a_high, a_low = a if isinstance(a, tuple) else split(a)
    b_high, b_low = b if isinstance(b, tuple) else split(b)
    (a_axis,), (b_axis,) = dims[0]
    return dot(
        jnp.concatenate([a_high, a_low, a_high], axis=a_axis),
        jnp.concatenate([b_high, b_high, b_low], axis=b_axis),
        dims,
    )


def normalize(values):
    center = values - jnp.mean(values, axis=-1, keepdims=True)
    spread = jnp.mean(center * center, axis=-1, keepdims=True)
    scale = lax.rsqrt(spread + 1e-05)
    return center * scale, scale


def normalize_back(grad, normed, scale):
    grad_mean = jnp.mean(grad, axis=-1, keepdims=True)
    along = jnp.mean(grad * normed, axis=-1, keepdims=True)
    return scale * (grad - grad_mean - normed * along)


def gate(values):
    return 0.5 + 0.5 * jnp.tanh(values * (K0 + K1 * (values * values)))


def gelu(values):
    return values * gate(values)


def gelu_slope(values, gated):
    return gated + 2.0 * values * (gated - gated * gated) * (K0 + (3.0 * K1) * (values * values))


def call(body, grid, in_specs, out_specs, out_shape, scratch=(), flops=0, bytes_accessed=0, limit=22):
    return pl.pallas_call(
        body,
        grid=grid,
        in_specs=in_specs,
        out_specs=out_specs,
        out_shape=out_shape,
        scratch_shapes=list(scratch),
        compiler_params=pltpu.CompilerParams(vmem_limit_bytes=limit * 2**20),
        cost_estimate=pl.CostEstimate(
            flops=flops, bytes_accessed=bytes_accessed, transcendentals=0
        ),
    )


def shape(*dims):
    return jax.ShapeDtypeStruct(dims, F32)


def whole(*dims):
    return pl.BlockSpec(dims, lambda *_: (0,) * len(dims))


def rows(*dims):
    return pl.BlockSpec(dims, lambda i: (i,) + (0,) * (len(dims) - 1))


def load_row(ref, lead, cols):
    return [ref[lead + (pl.ds(k, cols // 8, stride=8),)] for k in range(8)]


def load_rows(ref, cols):
    return jnp.concatenate(
        [part for i in range(ref.shape[0]) for part in load_row(ref, (i,), cols)], axis=0
    )


def fill_row(padded, at, row, left, right):
    cols = row.shape[0]
    padded[at, 8 : 8 + cols, :] = row
    padded[at, 0:1, :] = left
    padded[at, 1:8, :] = row[cols - 8 : cols - 1]
    padded[at, 8 + cols : 15 + cols, :] = row[1:8]
    padded[at, 15 + cols : 16 + cols, :] = right


def keep_row(values, flag):
    return jnp.where(flag > 0, values, 0.0)


def keep_column(values, flag, above, below):
    at = lax.broadcasted_iota(jnp.int32, values.shape, 0)
    kept = jnp.where(at == 0, above, jnp.where(at == values.shape[0] - 1, below, 1)) * flag
    return jnp.where(kept > 0, values, 0.0)


def forward_body(
    inside_ref, field_ref, late_ref, top_ref, bottom_ref, left_ref, right_ref, expand_ref, depth_ref, weight_ref,
    sent_ref, pre_ref, depth_out_ref, depth_top_ref, depth_bottom_ref, depth_left_ref, depth_right_ref,
    padded, left, right,
):
    step = pl.program_id(0)
    last = pl.num_programs(0) - 1
    count, cols, channels = field_ref.shape
    wide = expand_ref.shape[1]
    total_rows = padded.shape[0] - 2

    @pl.when(step == 0)
    def _():
        weight = split(expand_ref[...])

        def hidden(values):
            return gelu(dot3(normalize(values)[0], weight, NN))

        above, below = inside_ref[0], inside_ref[1]
        left[...] = hidden(keep_column(left_ref[...], inside_ref[2], above, below))
        right[...] = hidden(keep_column(right_ref[...], inside_ref[3], above, below))
        for at, ref, flag in ((0, top_ref, above), (total_rows + 1, bottom_ref, below)):
            row = hidden(keep_row(jnp.concatenate(load_row(ref, (), cols), axis=0), flag))
            fill_row(padded, at, row, left[at : at + 1, :], right[at : at + 1, :])

    @pl.when(step < last)
    def _():
        normed, _ = normalize(load_rows(field_ref, cols))
        pre = dot3(normed, expand_ref[...], NN)
        pre_ref[...] = pre.reshape(count, cols, wide)
        hidden = gelu(pre)
        for i in range(count):
            at = step * count + i + 1
            row = hidden[i * cols : (i + 1) * cols]
            fill_row(padded, at, row, left[pl.ds(at, 1), :], right[pl.ds(at, 1), :])

    @pl.when(step > 0)
    def _():
        start = (step - 1) * count
        for lane in range(0, wide, 128):
            lanes = slice(lane, lane + 128)
            for i in range(count):
                total = None
                for p in range(3):
                    for q in range(3):
                        term = padded[start + i + p, 8 * q : 8 * q + cols, lanes] * depth_ref[3 * p + q : 3 * p + q + 1, lanes]
                        total = term if total is None else total + term
                depth_out_ref[i, :, lanes] = total
        depth_left_ref[...] = depth_out_ref[:, 0, :]
        depth_right_ref[...] = depth_out_ref[:, cols - 1, :]
        activated = gelu(depth_out_ref[...].reshape(count * cols, wide))
        mixed = dot3(activated, weight_ref[...], NN) + load_rows(late_ref, cols)
        span = total_rows // GRID
        for i in range(count):
            block, inner = divmod(i, span)
            for k in range(8):
                here = i * cols + k * (cols // 8)
                sent_ref[block, pl.ds(inner * 8 + k, cols // 8, stride=span * 8), :] = mixed[
                    here : here + cols // 8
                ]

    @pl.when(step == 1)
    def _():
        depth_top_ref[...] = depth_out_ref[0]

    @pl.when(step == last)
    def _():
        depth_bottom_ref[...] = depth_out_ref[count - 1]


def forward(flags, field, halo, expand_weight, depth_weight, weight, count=8):
    tile_rows, tile_cols, channels = field.shape
    wide = expand_weight.shape[1]
    span = tile_rows // GRID
    steps = tile_rows // count
    edge = tile_rows + 2

    def early(*dims):
        return pl.BlockSpec(dims, lambda i: (jnp.minimum(i, steps - 1),) + (0,) * (len(dims) - 1))

    def late(*dims):
        return pl.BlockSpec(dims, lambda i: (jnp.maximum(i - 1, 0),) + (0,) * (len(dims) - 1))

    return call(
        forward_body,
        (steps + 1,),
        [pl.BlockSpec(memory_space=pltpu.SMEM), early(count, tile_cols, channels), late(count, tile_cols, channels)]
        + [whole(tile_cols, channels)] * 2
        + [whole(edge, channels)] * 2
        + [whole(channels, wide), whole(9, wide), whole(wide, channels)],
        [
            late(count // span, span * tile_cols, channels),
            early(count, tile_cols, wide),
            late(count, tile_cols, wide),
            whole(tile_cols, wide),
            whole(tile_cols, wide),
            late(count, wide),
            late(count, wide),
        ],
        [
            shape(GRID, span * tile_cols, channels),
            pltpu.HBM((tile_rows, tile_cols, wide), F32),
            pltpu.HBM((tile_rows, tile_cols, wide), F32),
            pltpu.HBM((tile_cols, wide), F32),
            pltpu.HBM((tile_cols, wide), F32),
            pltpu.HBM((tile_rows, wide), F32),
            pltpu.HBM((tile_rows, wide), F32),
        ],
        scratch=[
            pltpu.VMEM((edge, tile_cols + 16, wide), F32),
            pltpu.VMEM((edge, wide), F32),
            pltpu.VMEM((edge, wide), F32),
        ],
        flops=12 * tile_rows * tile_cols * channels * wide,
        bytes_accessed=4 * tile_rows * tile_cols * (2 * wide + 3 * channels),
    )(flags, field, field, *halo, expand_weight, depth_weight, weight)


def arrange_body(tile_ref, sent_ref):
    tile_rows, cols, _ = tile_ref.shape
    span = tile_rows // GRID
    for i in range(tile_rows):
        block, inner = divmod(i, span)
        for c in range(cols // 8):
            there = c * span * 8 + inner * 8
            sent_ref[block, there : there + 8, :] = tile_ref[i, 8 * c : 8 * c + 8, :]


def arrange(tile):
    tile_rows, tile_cols, channels = tile.shape
    vmem = pl.BlockSpec(memory_space=pltpu.VMEM)
    return call(arrange_body, (), [vmem], vmem, shape(GRID, tile_rows * tile_cols // GRID, channels))(tile)


SPARE = 8


def pitched(ref, lead, first, count, pitch, groups):
    return jnp.concatenate(
        [ref[lead + (pl.ds(pl.multiple_of((first + j) * pitch, 8), groups),)] for j in range(count)], axis=0
    )


def attend_body(
    mixed_ref, cot_ref, qkv_ref, out_ref, bias_ref,
    leave_ref, mixture_out, grad_packed_out, grad_bias_out,
    packed_ref, delta_ref, mixture_ref, grad_packed_ref, bias_total, grad_bias_ref, done,
):
    places, groups, channels = mixed_ref.shape
    head = channels // HEADS
    scale = head ** (-0.5)
    pitch = groups + SPARE
    step = 32
    rows_in = step * groups
    together = 8

    def chunk(i, ref):
        return ref[pl.ds(i * step, step)].reshape(rows_in, channels)

    def prepare(i, carry):
        normed, _ = normalize(chunk(i, mixed_ref))
        packed = dot3(normed, qkv_ref[...], NN)
        delta = dot3(chunk(i, cot_ref), out_ref[...], NT)
        for j in range(step):
            here = pl.ds(pl.multiple_of((i * step + j) * pitch, 8), groups)
            part = slice(j * groups, (j + 1) * groups)
            packed_ref[0, here, :] = packed[part, :channels] * scale
            packed_ref[1, here, :] = packed[part, channels : 2 * channels]
            packed_ref[2, here, :] = packed[part, 2 * channels :]
            delta_ref[here, :] = delta[part]
        return carry

    lax.fori_loop(0, places // step, prepare, 0)
    bias_total[...] = jnp.zeros_like(bias_total)

    head_of = lax.broadcasted_iota(jnp.int32, (places, channels), 1) // head

    def spread(values):
        return jnp.concatenate(
            [jnp.where(head_of == h, values, 0.0).astype(BF16) for h in range(HEADS)], axis=0
        )

    def spread_split(values):
        high, low = split(values)
        return spread(high.astype(F32)), spread(low.astype(F32))

    def gather_heads(wide):
        total = jnp.where(head_of == 0, wide[:places], 0.0)
        for h in range(1, HEADS):
            total = total + jnp.where(head_of == h, wide[h * places : (h + 1) * places], 0.0)
        return total

    def some_groups(i, carry):
        here = [pl.ds(i * together + k, places, stride=pitch) for k in range(together)]
        query = [spread_split(packed_ref[0, h, :]) for h in here]
        delta = [spread_split(delta_ref[h, :]) for h in here]
        key = [split(packed_ref[1, h, :]) for h in here]
        value = [split(packed_ref[2, h, :]) for h in here]
        scores = [dot3(a, b, NT) + bias_ref[...] for a, b in zip(key, query)]
        grad_weights = [dot3(a, b, NT) for a, b in zip(value, delta)]
        powers = [jnp.exp(s - jnp.max(s, axis=0, keepdims=True)) for s in scores]
        weights = [p * (1.0 / jnp.sum(p, axis=0, keepdims=True)) for p in powers]
        along = [jnp.sum(w * g, axis=0, keepdims=True) for w, g in zip(weights, grad_weights)]
        grad_scores = [w * (g - a) for w, g, a in zip(weights, grad_weights, along)]
        weights = [split(w) for w in weights]
        grad_split = [split(g) for g in grad_scores]
        mixture = [gather_heads(dot3(w, v, TN)) for w, v in zip(weights, value)]
        grad_value = [dot3(w, d, NN) for w, d in zip(weights, delta)]
        grad_key = [dot3(g, q, NN) for g, q in zip(grad_split, query)]
        grad_query = [gather_heads(dot3(g, k, TN)) * scale for g, k in zip(grad_split, key)]
        for k, h in enumerate(here):
            mixture_ref[h, :] = mixture[k]
            grad_packed_ref[0, h, :] = grad_query[k]
            grad_packed_ref[1, h, :] = grad_key[k]
            grad_packed_ref[2, h, :] = grad_value[k]
        bias_total[...] += functools.reduce(jnp.add, grad_scores)
        return carry

    lax.fori_loop(0, groups // together, some_groups, 0)

    half = bias_total.shape[1] // 2
    grad_bias_ref[:places, :] = bias_total[:, :half]
    grad_bias_ref[places:, :] = bias_total[:, half:]
    copies = [
        pltpu.make_async_copy(mixture_ref, mixture_out, done.at[0]),
        pltpu.make_async_copy(grad_packed_ref, grad_packed_out, done.at[1]),
        pltpu.make_async_copy(grad_bias_ref, grad_bias_out, done.at[2]),
    ]
    for copy in copies:
        copy.start()

    def finish(i, carry):
        normed, spread_scale = normalize(chunk(i, mixed_ref))
        grad = jnp.concatenate(
            [pitched(grad_packed_ref, (k,), i * step, step, pitch, groups) for k in range(3)], axis=1
        )
        grad_in = normalize_back(dot3(grad, qkv_ref[...], NT), normed, spread_scale)
        leave_ref[pl.ds(i * step, step)] = grad_in.reshape(step, groups, channels)
        return carry

    lax.fori_loop(0, places // step, finish, 0)
    for copy in copies:
        copy.wait()


def attend(mixed, cot, qkv_weight, out_weight, bias):
    places, groups, channels = mixed.shape
    tokens = places * groups
    padded = places * (groups + SPARE)
    vmem = pl.BlockSpec(memory_space=pltpu.VMEM)
    return call(
        attend_body,
        (),
        [vmem] * 5,
        [vmem] + [pl.BlockSpec(memory_space=pl.ANY)] * 3,
        [
            shape(places, groups, channels), pltpu.HBM((padded, channels), F32), pltpu.HBM((3, padded, channels), F32),
            pltpu.HBM((2 * places, bias.shape[1] // 2), F32),
        ],
        scratch=[
            pltpu.VMEM((3, padded, channels), F32),
            pltpu.VMEM((padded, channels), F32),
            pltpu.VMEM((padded, channels), F32),
            pltpu.VMEM((3, padded, channels), F32),
            pltpu.VMEM(bias.shape, F32),
            pltpu.VMEM((2 * places, bias.shape[1] // 2), F32),
            pltpu.SemaphoreType.DMA((3,)),
        ],
        flops=6 * tokens * channels * (12 * channels + 6 * places),
        bytes_accessed=16 * tokens * channels,
    )(mixed, cot, qkv_weight, out_weight, bias)


def attend_late_body(
    mixed_ref, cot_ref, mixture_ref, grad_packed_ref, out_ref, attended_ref, grad_qkv_ref, grad_out_ref
):
    @pl.when(pl.program_id(0) == 0)
    def _():
        grad_qkv_ref[...] = jnp.zeros_like(grad_qkv_ref)
        grad_out_ref[...] = jnp.zeros_like(grad_out_ref)

    step, groups, channels = mixed_ref.shape
    pitch = groups + SPARE
    mixture = split(pitched(mixture_ref, (), 0, step, pitch, groups))
    attended_ref[...] = dot3(mixture, out_ref[...], NN).reshape(attended_ref.shape)
    grad_out_ref[...] += dot3(mixture, cot_ref[...].reshape(step * groups, channels), TN)
    normed, _ = normalize(mixed_ref[...].reshape(step * groups, channels))
    grad = jnp.concatenate(
        [pitched(grad_packed_ref, (k,), 0, step, pitch, groups) for k in range(3)], axis=1
    )
    grad_qkv_ref[...] += dot3(normed, grad, TN)


def attend_late(mixed, cot, mixture, grad_packed, out_weight, step=16):
    places, groups, channels = mixed.shape
    tile = rows(step, groups, channels)
    return call(
        attend_late_body,
        (places // step,),
        [
            tile, tile, rows(step * (groups + SPARE), channels),
            pl.BlockSpec((3, step * (groups + SPARE), channels), lambda i: (0, i, 0)), whole(channels, channels),
        ],
        [tile, whole(channels, 3 * channels), whole(channels, channels)],
        [shape(places, groups, channels), shape(channels, 3 * channels), shape(channels, channels)],
        flops=30 * places * groups * channels * channels,
        bytes_accessed=28 * places * groups * channels,
    )(mixed, cot, mixture, grad_packed, out_weight)


def edges_body(
    came_ref, cot_ref, top_ref, bottom_ref, left_ref, right_ref, weight_ref,
    grad_top_ref, grad_bottom_ref, grad_left_ref, grad_right_ref, mixed,
):
    tile_rows, cols, _ = cot_ref.shape
    span = tile_rows // GRID
    piece = span * 8
    sides = 2 * cols
    for at, i in ((0, 0), (cols, tile_rows - 1)):
        block, inner = divmod(i, span)
        for k in range(8):
            here = at + k * (cols // 8)
            mixed[here : here + cols // 8] = (
                came_ref[block, pl.ds(inner * 8 + k, cols // 8, stride=piece), :]
                + cot_ref[i, pl.ds(k, cols // 8, stride=8), :]
            )
    for at, j in ((sides, 0), (sides + tile_rows, cols - 1)):
        first = (j // 8) * piece + j % 8
        for block in range(GRID):
            mixed[at + block * span : at + (block + 1) * span] = came_ref[block, pl.ds(first, span, stride=8), :]
        mixed[at : at + tile_rows] += cot_ref[:, j, :]
    grad = dot3(mixed[...], weight_ref[...], NT)
    at = 0
    for depth_ref, grad_ref in (
        (top_ref, grad_top_ref), (bottom_ref, grad_bottom_ref), (left_ref, grad_left_ref), (right_ref, grad_right_ref)
    ):
        depth_out = depth_ref[...]
        grad_ref[...] = grad[at : at + depth_out.shape[0]] * gelu_slope(depth_out, gate(depth_out))
        at += depth_out.shape[0]


def edges(came, cot, depth_edges, weight):
    tile_rows, tile_cols, channels = cot.shape
    wide = weight.shape[0]
    vmem = pl.BlockSpec(memory_space=pltpu.VMEM)
    return call(
        edges_body,
        (),
        [vmem] * 7,
        [vmem] * 4,
        [shape(*a.shape) for a in depth_edges],
        scratch=[pltpu.VMEM((2 * tile_cols + 2 * tile_rows, channels), F32)],
        flops=12 * (tile_cols + tile_rows) * channels * wide,
        bytes_accessed=2**21,
        limit=56,
    )(came, cot, *depth_edges, weight)


def project_back_body(
    came_ref, cot_ref, depth_out_ref, weight_ref,
    grad_mixed_ref, grad_depth_ref, total_ref,
):
    step = pl.program_id(0)
    count, cols, wide = depth_out_ref.shape
    span = count // came_ref.shape[0]
    piece = span * 8

    @pl.when(step == 0)
    def _():
        total_ref[...] = jnp.zeros_like(total_ref)

    parts = []
    for i in range(count):
        block, inner = divmod(i, span)
        for k, cot in enumerate(load_row(cot_ref, (i,), cols)):
            parts.append(came_ref[block, pl.ds(inner * 8 + k, cols // 8, stride=piece), :] + cot)
    grad_mixed = jnp.concatenate(parts, axis=0)
    grad_mixed_ref[...] = grad_mixed.reshape(grad_mixed_ref.shape)
    mixed_split = split(grad_mixed)
    depth_out = depth_out_ref[...].reshape(count * cols, wide)
    gated = gate(depth_out)
    grad = dot3(mixed_split, weight_ref[...], NT) * gelu_slope(depth_out, gated)
    grad_depth_ref[...] = grad.reshape(count, cols, wide)
    total_ref[...] += dot3(mixed_split, depth_out * gated, TN)


def project_back(came, cot, depth_out, weight, count=8):
    tile_rows, tile_cols, wide = depth_out.shape
    channels = weight.shape[1]
    span = tile_rows // GRID
    tile = rows(count, tile_cols, channels)
    return call(
        project_back_body,
        (tile_rows // count,),
        [rows(count // span, span * tile_cols, channels), tile, rows(count, tile_cols, wide), whole(wide, channels)],
        [tile, rows(count, tile_cols, wide), whole(channels, wide)],
        [shape(tile_rows, tile_cols, channels), shape(tile_rows, tile_cols, wide), shape(channels, wide)],
        flops=12 * tile_rows * tile_cols * channels * wide,
        bytes_accessed=4 * tile_rows * tile_cols * (2 * wide + 3 * channels),
        limit=56,
    )(came, cot, depth_out, weight)


SLOTS = 16


def pack(refs, taps_ref, target, half):
    size = refs[0].shape[0] // 2
    own = pl.ds(pl.multiple_of(half * size, size), size)
    slot = 0
    for ref in refs:
        for lane in range(0, ref.shape[1], 2 * size):
            target[pl.ds(slot, size, stride=SLOTS), :] = ref[own, lane : lane + 2 * size]
            slot += 1
    target[pl.ds(slot, size, stride=SLOTS), :] = taps_ref[own, :]
    for spare in range(slot + 1, SLOTS):
        target[pl.ds(spare, size, stride=SLOTS), :] = jnp.zeros((size, 2 * size), F32)


def expand_back_body(
    inside_ref, grad_ref, before_ref, after_ref, top, bottom, left_ref, right_ref, pre_ref, field_ref, depth_ref,
    project_ref, qkv_ref, out_ref, bias_ref,
    grad_pre_ref, kept_ref, given_ref, padded, left, right, grad_expand_ref, grad_depth_ref, taps_ref,
):
    step = pl.program_id(0)
    last = pl.num_programs(0) - 1
    count, cols, wide = grad_ref.shape

    @pl.when(step == 0)
    def _():
        grad_expand_ref[...] = jnp.zeros_like(grad_expand_ref)
        grad_depth_ref[...] = jnp.zeros_like(grad_depth_ref)
        left[...] = keep_column(left_ref[...], inside_ref[2], inside_ref[0], inside_ref[1])
        right[...] = keep_column(right_ref[...], inside_ref[3], inside_ref[0], inside_ref[1])

    def fill(at, row):
        edge = pl.ds(step * count + at, 1)
        fill_row(padded, at, row, left[edge, :], right[edge, :])

    fill(0, jnp.where(step == 0, keep_row(top[...], inside_ref[0]), before_ref[0]))
    fill(count + 1, jnp.where(step == last, keep_row(bottom[...], inside_ref[1]), after_ref[0]))
    for i in range(count):
        fill(i + 1, grad_ref[i])
    for lane in range(0, wide, 128):
        lanes = slice(lane, lane + 128)
        taps = [None] * 9
        for i in range(count):
            pre = pre_ref[i, :, lanes]
            gated = gate(pre)
            hidden = pre * gated
            total = None
            for tap in range(9):
                p, q = divmod(tap, 3)
                window = padded[i + 2 - p, 8 * (2 - q) : 8 * (2 - q) + cols, lanes]
                term = window * depth_ref[tap : tap + 1, lanes]
                total = term if total is None else total + term
                part = jnp.sum((window * hidden).reshape(cols // 8, 8, 128), axis=0)
                taps[tap] = part if taps[tap] is None else taps[tap] + part
            grad_pre_ref[i, :, lanes] = total * gelu_slope(pre, gated)
        for tap in range(9):
            grad_depth_ref[tap : tap + 1, lanes] += jnp.sum(taps[tap], axis=0, keepdims=True)
    normed, _ = normalize(load_rows(field_ref, cols))
    grad_expand_ref[...] += dot3(normed, grad_pre_ref[...].reshape(count * cols, wide), TN)

    @pl.when(step == last)
    def _():
        taps_ref[...] = jnp.zeros_like(taps_ref)
        taps, size = grad_depth_ref.shape[0], taps_ref.shape[1]
        for k in range(wide // size):
            taps_ref[k * taps : (k + 1) * taps, :] = grad_depth_ref[:, k * size : (k + 1) * size]
        refs = (grad_expand_ref, project_ref, qkv_ref, out_ref, bias_ref)
        pack(refs, taps_ref, kept_ref, inside_ref[4])
        pack(refs, taps_ref, given_ref, 1 - inside_ref[4])


def expand_back(flags, grad_depth_out, halo, pre, field, depth_weight, grads, count=8):
    tile_rows, tile_cols, channels = field.shape
    wide = pre.shape[2]
    edge = tile_rows + 2
    return call(
        expand_back_body,
        (tile_rows // count,),
        [
            pl.BlockSpec(memory_space=pltpu.SMEM),
            rows(count, tile_cols, wide),
            pl.BlockSpec((1, tile_cols, wide), lambda i: (jnp.maximum(count * i - 1, 0), 0, 0)),
            pl.BlockSpec((1, tile_cols, wide), lambda i: (jnp.minimum(count * i + count, tile_rows - 1), 0, 0)),
        ]
        + [whole(tile_cols, wide)] * 2
        + [whole(edge, wide)] * 2
        + [rows(count, tile_cols, wide), rows(count, tile_cols, channels), whole(9, wide)]
        + [whole(*a.shape) for a in grads],
        [rows(count, tile_cols, wide)] + [whole(channels // 2 * SLOTS, channels)] * 2,
        [pltpu.HBM((tile_rows, tile_cols, wide), F32)] + [shape(channels // 2 * SLOTS, channels)] * 2,
        scratch=[
            pltpu.VMEM((count + 2, tile_cols + 16, wide), F32),
            pltpu.VMEM((edge, wide), F32),
            pltpu.VMEM((edge, wide), F32),
            pltpu.VMEM((channels, wide), F32),
            pltpu.VMEM((16, wide), F32),
            pltpu.VMEM((channels, channels), F32),
        ],
        flops=6 * tile_rows * tile_cols * channels * wide,
        bytes_accessed=4 * tile_rows * tile_cols * (3 * wide + channels),
        limit=56,
    )(flags, grad_depth_out, grad_depth_out, grad_depth_out, *halo, pre, field, depth_weight, *grads)


def finish_body(
    grad_pre_ref, field_ref, grad_mixed_ref, sent_ref, placed_ref, expand_ref, block_out_ref, grad_field_ref
):
    count, cols, wide = grad_pre_ref.shape
    span = count // sent_ref.shape[0]
    for i in range(count):
        block, inner = divmod(i, span)
        for c in range(cols // 8):
            there = slice(c * span * 8 + inner * 8, c * span * 8 + inner * 8 + 8)
            block_out_ref[i, 8 * c : 8 * c + 8, :] = sent_ref[block, there, :] + placed_ref[block, there, :]
    normed, scale = normalize(load_rows(field_ref, cols))
    grad_normed = dot3(grad_pre_ref[...].reshape(count * cols, wide), expand_ref[...], NT)
    grad_field = normalize_back(grad_normed, normed, scale) + grad_mixed_ref[...].reshape(count * cols, -1)
    for i in range(count):
        for k in range(8):
            here = i * cols + k * (cols // 8)
            grad_field_ref[i, pl.ds(k, cols // 8, stride=8), :] = grad_field[here : here + cols // 8]


def finish(grad_pre, field, grad_mixed, sent, placed, expand_weight, count=8):
    tile_rows, tile_cols, channels = field.shape
    wide = grad_pre.shape[2]
    span = tile_rows // GRID
    tile = rows(count, tile_cols, channels)
    blocks = rows(count // span, span * tile_cols, channels)
    return call(
        finish_body,
        (tile_rows // count,),
        [rows(count, tile_cols, wide), tile, tile, blocks, blocks, whole(channels, wide)],
        [tile, tile],
        [shape(*field.shape)] * 2,
        flops=6 * tile_rows * tile_cols * channels * wide,
        bytes_accessed=4 * tile_rows * tile_cols * (wide + 6 * channels),
        limit=56,
    )(grad_pre, field, grad_mixed, sent, placed, expand_weight)


def add_body(first_ref, second_ref, sum_ref):
    sum_ref[...] = first_ref[...] + second_ref[...]


def total_body(came_ref, total_ref):
    total = jnp.sum(came_ref[...], axis=0, keepdims=True)
    total_ref[...] = jnp.broadcast_to(total, total_ref.shape)


def unpack_body(inside_ref, mine_ref, other_ref, expand_ref, project_ref, qkv_ref, out_ref, bias_ref, depth_ref):
    size = out_ref.shape[0]
    places = bias_ref.shape[1]

    def matrix(slot):
        here = pl.ds(slot, size // 2, stride=SLOTS)
        mine, other = mine_ref[here, :], other_ref[here, :]
        second = inside_ref[4] > 0
        return jnp.concatenate([jnp.where(second, other, mine), jnp.where(second, mine, other)], axis=0)

    slot = 0
    for k in range(expand_ref.shape[1] // size):
        expand_ref[:, k * size : (k + 1) * size] = matrix(slot)
        slot += 1
    for k in range(project_ref.shape[0] // size):
        project_ref[k * size : (k + 1) * size, :] = matrix(slot).T
        slot += 1
    for k in range(qkv_ref.shape[1] // size):
        qkv_ref[:, k * size : (k + 1) * size] = matrix(slot)
        slot += 1
    out_ref[...] = matrix(slot)
    bias = matrix(slot + 1)
    for h in range(HEADS):
        at, lane = divmod(h, 2)
        bias_ref[h] = bias[at * places : (at + 1) * places, lane * places : (lane + 1) * places].T
    taps = matrix(slot + 2)
    for k in range(depth_ref.shape[1] // size):
        depth_ref[:, k * size : (k + 1) * size] = taps[16 * k : 16 * k + depth_ref.shape[0]]


def reduce_all(flags, kept, given, like, after, beside):
    size = kept.shape[1]
    chips = size // 2
    vmem = pl.BlockSpec(memory_space=pltpu.VMEM)
    pair = [(0, 1), (1, 0)]
    own = call(add_body, (), [vmem] * 2, vmem, shape(*kept.shape))(kept, lax.ppermute(given, "core", pair))
    own, after = lax.optimization_barrier((own, after))
    came = lax.all_to_all(own.reshape(chips, SLOTS, size), PAIRS, 0, 0, tiled=True)
    total = call(total_body, (), [vmem], vmem, shape(chips, SLOTS, size))(came)
    mine = lax.all_to_all(total, PAIRS, 0, 0, tiled=True).reshape(chips * SLOTS, size)
    mine, others = lax.optimization_barrier((mine, beside(after)))
    other = lax.ppermute(mine, "core", pair)
    totals = call(
        unpack_body,
        (),
        [pl.BlockSpec(memory_space=pltpu.SMEM), vmem, vmem],
        [vmem] * 6,
        [shape(*a.shape) for a in like],
    )(flags, mine, other)
    return totals, others


def shift(values, axes, count, by):
    return lax.ppermute(values, axes, [(i, (i + by) % count) for i in range(count)])


def inside(row_count, col_count):
    row, col = lax.axis_index("row"), lax.axis_index(COLS)
    second = lax.axis_index("core") > 0
    return jnp.stack([row > 0, row < row_count - 1, col > 0, col < col_count - 1, second]).astype(jnp.int32)


def beyond_rows(first, last, row_count):
    return shift(last, "row", row_count, 1), shift(first, "row", row_count, -1)


def beyond_columns(top, bottom, left, right, col_count):
    def column(edge, j):
        return jnp.concatenate([top[j : j + 1], edge, bottom[j : j + 1]], axis=0)

    end = top.shape[0] - 1
    return shift(column(right, end), COLS, col_count, 1), shift(column(left, 0), COLS, col_count, -1)


def swap(blocks):
    places = GRID * GRID
    flat = blocks.reshape(places, -1, blocks.shape[-1])
    return lax.all_to_all(flat, PAIRS, 0, 0, tiled=True)


def on_device(
    sizes, field, expand_weight, depth_weight, project_weight, qkv_weight, out_weight, pos_bias, cotangent
):
    places = GRID * GRID
    row_count, col_count = sizes
    flags = inside(row_count, col_count)
    halo = beyond_rows(field[0], field[-1], row_count)
    halo += beyond_columns(*halo, field[:, 0], field[:, -1], col_count)
    arranged, halo = lax.optimization_barrier((arrange(cotangent), halo))
    cot_grid = swap(arranged)
    sent, pre, depth_out, *depth_edges = forward(flags, field, halo, expand_weight, depth_weight, project_weight)
    mixed_grid = swap(sent)
    bias = pos_bias.transpose(2, 0, 1).reshape(places, HEADS * places)
    leave, mixture, grad_packed, grad_bias = attend(mixed_grid, cot_grid, qkv_weight, out_weight, bias)
    came = swap(leave)
    attended, grad_qkv, grad_out = attend_late(mixed_grid, cot_grid, mixture, grad_packed, out_weight)
    came, attended = lax.optimization_barrier((came, attended))
    came = came.reshape(sent.shape)
    first, last, left, right = edges(came, cotangent, depth_edges, project_weight)
    halo = beyond_rows(first, last, row_count)
    grad_mixed, grad_depth_out, grad_project = project_back(came, cotangent, depth_out, project_weight)
    halo, grad_depth_out = lax.optimization_barrier((halo, grad_depth_out))
    halo += beyond_columns(*halo, left, right, col_count)
    halo, attended = lax.optimization_barrier((halo, attended))
    placed = swap(attended).reshape(sent.shape)
    grad_pre, kept, given = expand_back(
        flags, grad_depth_out, halo, pre, field, depth_weight, (grad_project, grad_qkv, grad_out, grad_bias)
    )
    totals, (block_out, grad_field) = reduce_all(
        flags,
        kept,
        given,
        (expand_weight, project_weight, qkv_weight, out_weight, pos_bias, depth_weight),
        placed,
        lambda placed: finish(grad_pre, field, grad_mixed, sent, placed, expand_weight),
    )
    grad_expand, grad_project, grad_qkv, grad_out, grad_bias, grad_depth = totals
    return (
        block_out,
        grad_field,
        grad_expand,
        grad_depth,
        grad_project,
        grad_qkv,
        grad_out,
        grad_bias,
    )


def solution(mesh):
    row_count, col_count = mesh.devices.shape
    split_mesh = Mesh(mesh.devices.reshape(row_count, col_count // 2, 2), ALL)
    tile = P("row", COLS, None)
    return jax.shard_map(
        functools.partial(on_device, (row_count, col_count)),
        mesh=split_mesh,
        in_specs=(tile, P(), P(), P(), P(), P(), P(), tile),
        out_specs=(tile, tile, P(), P(), P(), P(), P(), P()),
        check_vma=False,
    )
```
